32 devices in a mesh: groups: 2 (over x), seq: 16 (over z, y, core).
Axes of the slice: x: 2, y: 2, z: 4, core: 2. Of those that a mesh axis runs over, the one named last changes fastest.
Arguments:
- x_stream: bfloat16 [4096, 8192], P(('groups', 'seq')), parts along dimension 0, may hold values from -6 to 6
- bc_stream: bfloat16 [4096, 2048], P(('groups', 'seq')), parts along dimension 0, may hold values from -6 to 6
- z_stream: bfloat16 [4096, 8192], P(('groups', 'seq')), parts along dimension 0, may hold values from -6 to 6
- dt_raw: bfloat16 [4096, 128], P(('groups', 'seq')), parts along dimension 0, may hold values from -3 to 5
- doc_ids: int32 [4096], P('groups'), parts along dimension 0, may hold values from 0 to 15, never falling along the last dimension, each value on 1 to 512 neighbouring positions
- conv_weight: float32 [4, 10240], replicated, may hold values from -3 to 3
- conv_bias: float32 [10240], replicated, may hold values from -1.8 to 1.8
- dt_bias: float32 [128], replicated, may hold values from -1 to 0.5
- a_log: float32 [128], replicated, may hold values from -8 to -2.5
- skip_d: float32 [128], replicated, may hold values from 0.5 to 1.5
- norm_gain: float32 [8192], replicated, may hold values from 0.5 to 1.5
Outputs:
- mixed: bfloat16 [4096, 8192], P(('groups', 'seq')), parts along dimension 0
- doc_cosine: float32 [32], P('groups'), parts along dimension 0
The draws below stay inside these ranges and needn't reach their ends.
There are 2 independent parts, one for each index of `groups`. The reference program is written for one: setup_inputs(seed, part) draws one part's arguments, and reference() takes and returns one part's arrays. A program takes and returns all parts, laid end to end along the dimension named above; an argument that names none is the same for every part. Nothing has to cross between parts.
Inputs may be any that keep to these rules, and one draw needn't show every extreme that they name: `doc_ids`: document ids never fall along the stream; every id is used, each document has at most 512 tokens and one has exactly that many.
All inputs are finite; a program needn't handle non-finite values.
Results may differ from the reference program's by a relative error of at most 0.0054.
Values may be sent and summed in bfloat16 or wider, within the bound.
No kernel may reach another device: no remote copies, remote signals or barrier semaphores. Data moves between devices by JAX's collectives and lax.ppermute only.
A program may use at most 128 MiB of HBM per device.

```python
import math
import jax
import jax.numpy as jnp
import numpy as np
from jax import lax

HEADS = 128
HDIM = 64
GROUPS = 4
STATE = 256
KERNEL = 4
SPAN = 512
DOCS = 16
TOKENS = 2048
DOC_MOST = 512
CHANNELS = 10240


def draw_dt_raw(key, part):
    key = jax.random.fold_in(key, 23)
    base_key, spot_key = jax.random.split(key)
    base = jnp.clip(0.8 * jax.random.normal(base_key, (TOKENS, HEADS), jnp.float32) - 0.3, -3.0, 2.0)
    spots = jax.random.randint(spot_key, (4,), 0, TOKENS)
    struck = jnp.any(jnp.arange(TOKENS)[:, None] == spots[None, :], axis=1)
    return jnp.where(struck[:, None], 5.0, base).astype(jnp.bfloat16)


def draw_a_log(key, part):
    key = jax.random.fold_in(key, 11)
    return jax.random.uniform(key, (HEADS,), jnp.float32, -8.0, -2.5)


def steps_of(key, shape, shards, low, high):
    level, own = 1.0, jax.random.fold_in(key, 6)
    for dim, shards_of in shards:
        heights = jnp.exp(jax.random.uniform(jax.random.fold_in(own, dim), (shards_of,), jnp.float32, low / len(shards), high / len(shards)))
        level = level * jnp.repeat(heights, shape[dim] // shards_of).reshape([-1 if axis == dim else 1 for axis in range(len(shape))])
    return level


def split_up(count, total, bound, skew):
    portions = [(1 << 20) // math.isqrt(rank ** skew) + 1 for rank in range(2, count + 1)]
    spare, counts = total - bound - (count - 1), [1] * (count - 1)
    while spare > 0:
        candidates = [i for i in range(count - 1) if counts[i] < bound]
        pool, budget = sum([portions[i] for i in candidates]), spare
        for i in candidates:
            extra = min(bound - counts[i], max(1, budget * portions[i] // pool), spare)
            counts[i] = counts[i] + extra
            spare = spare - extra
    return np.array([bound] + counts)


def ragged_sizes(key, amount, total, limit, lean):
    if amount == 2:
        one = jax.random.randint(key, (), max(1, total - limit), min(limit, total - 1) + 1)
        return jnp.stack([one, total - one])
    tallies = jnp.asarray(split_up(amount, total, limit, lean), jnp.int32)
    pairs = (amount - 1) // 2
    donor, taker = tallies[1:1 + 2 * pairs:2], tallies[2:2 + 2 * pairs:2]
    room = jnp.minimum(donor - 1, limit - taker)
    moved = jax.random.randint(jax.random.fold_in(key, 1), (pairs,), 0, 1 << 20) % (room + 1)
    tallies = tallies.at[1:1 + 2 * pairs:2].set(donor - moved).at[2:2 + 2 * pairs:2].set(taker + moved)
    return tallies[jax.random.permutation(jax.random.fold_in(key, 2), amount)]


def noise(own_key, shape, width, limit, shards=(), held_as=jnp.bfloat16):
    drawn = width * jax.random.normal(own_key, shape, jnp.float32)
    if shards:
        drawn = drawn * steps_of(own_key, shape, shards, -0.22, 0.18)
    return jnp.clip(drawn, -limit, limit).astype(held_as)


def setup_inputs(seed: int = 0, part: int = 0) -> dict:
    key_of = jax.random.split(jax.random.key(seed), 12)
    part_keys = jax.random.split(jax.random.fold_in(key_of[11], part), 12)
    x_stream = noise(part_keys[0], (TOKENS, HEADS * HDIM), 1.0, 6.0, ((0, 16),))
    bc_stream = noise(part_keys[1], (TOKENS, 2 * GROUPS * STATE), 1.0, 6.0, ((0, 16),))
    z_stream = noise(part_keys[2], (TOKENS, HEADS * HDIM), 1.0, 6.0, ((0, 16),))
    dt_raw = draw_dt_raw(jax.random.fold_in(jax.random.fold_in(key_of[11], part), 71), part)
    doc_ids = jnp.searchsorted(jnp.cumsum(ragged_sizes(part_keys[4], DOCS, TOKENS, DOC_MOST, 2)), jnp.arange(TOKENS), side="right").astype(jnp.int32)
    conv_weight = noise(key_of[5], (KERNEL, CHANNELS), 0.5, 3.0, (), jnp.float32)
    conv_bias = noise(key_of[6], (CHANNELS,), 0.3, 1.8, (), jnp.float32)
    dt_bias = jnp.clip(jax.random.uniform(key_of[7], (HEADS,), jnp.float32, -1.0, 0.5), -1.0, 0.5)
    a_log = draw_a_log(jax.random.fold_in(key_of[11], 71), part)
    skip_d = jnp.clip(jax.random.uniform(key_of[9], (HEADS,), jnp.float32, 0.5, 1.5), 0.5, 1.5)
    norm_gain = jnp.clip(1.0 + 0.1 * jax.random.normal(key_of[10], (HEADS * HDIM,), jnp.float32), 0.5, 1.5)
    return dict(x_stream=x_stream, bc_stream=bc_stream, z_stream=z_stream, dt_raw=dt_raw, doc_ids=doc_ids, conv_weight=conv_weight, conv_bias=conv_bias, dt_bias=dt_bias, a_log=a_log, skip_d=skip_d, norm_gain=norm_gain)


def causal_conv(extended, ext_docs, weight, bias, row_count):
    kernel_taps = weight.shape[0]
    own_docs = ext_docs[kernel_taps - 1:]
    summed = jnp.zeros((row_count, extended.shape[1]), jnp.float32)
    for offset in range(kernel_taps):
        shifted = lax.slice_in_dim(extended, offset, offset + row_count, axis=0).astype(jnp.float32)
        same_doc = (lax.slice_in_dim(ext_docs, offset, offset + row_count, axis=0) == own_docs).astype(jnp.float32)
        summed = summed + weight[offset][None, :] * shifted * same_doc[:, None]
    return jax.nn.silu(summed + bias[None, :]).astype(jnp.bfloat16)

def gated_norm(y_rows, z_rows, gain, group_count):
    row_count = y_rows.shape[0]
    gated = y_rows.astype(jnp.float32) * jax.nn.silu(z_rows.astype(jnp.float32))
    gated = gated.reshape(row_count, group_count, -1)
    scale = lax.rsqrt(lax.optimization_barrier(jnp.mean(gated * gated, axis=-1, keepdims=True)) + 1e-05)
    return (gated * scale * gain.reshape(group_count, -1)[None]).reshape(row_count, -1).astype(jnp.bfloat16)

def reference(x_stream, bc_stream, z_stream, dt_raw, doc_ids, conv_weight, conv_bias, dt_bias, a_log, skip_d, norm_gain):
    inner_width = HEADS * HDIM
    pad_docs = jnp.concatenate([jnp.full((KERNEL - 1,), -1, jnp.int32), doc_ids.astype(jnp.int32)])
    x_ext = jnp.concatenate([jnp.zeros((KERNEL - 1, inner_width), jnp.bfloat16), x_stream])
    bc_ext = jnp.concatenate([jnp.zeros((KERNEL - 1, 2 * GROUPS * STATE), jnp.bfloat16), bc_stream])
    x_conv = causal_conv(x_ext, pad_docs, conv_weight[:, :inner_width], conv_bias[:inner_width], TOKENS)
    bc_conv = causal_conv(bc_ext, pad_docs, conv_weight[:, inner_width:], conv_bias[inner_width:], TOKENS)
    b_all = bc_conv[:, :GROUPS * STATE].reshape(TOKENS, GROUPS, STATE)
    c_all = bc_conv[:, GROUPS * STATE:].reshape(TOKENS, GROUPS, STATE)
    step_size = jax.nn.softplus(dt_raw.astype(jnp.float32) + dt_bias[None, :])
    log_rate = -jnp.exp(a_log)[None, :] * step_size
    span_count = TOKENS // SPAN
    cum_all = jnp.cumsum(log_rate.reshape(span_count, SPAN, HEADS), axis=1)
    repeat_count = HEADS // GROUPS

    def span_step(carry, block_data):
        carry_state, prev_doc = carry
        x_span, b_span, c_span, dt_span, cum_span, seg_span = block_data
        span_len = x_span.shape[0]
        row_index = lax.broadcasted_iota(jnp.int32, (span_len, span_len), 0)
        col_index = lax.broadcasted_iota(jnp.int32, (span_len, span_len), 1)
        same_mask = (seg_span[:, None] == seg_span[None, :]) & (row_index >= col_index)
        scores = jnp.einsum('igs,jgs->gij', c_span.astype(jnp.float32), b_span.astype(jnp.float32), precision=lax.Precision.HIGHEST)
        scores = jnp.repeat(scores, repeat_count, axis=0)
        cum_heads = jnp.transpose(cum_span)
        gaps_log = cum_heads[:, :, None] - cum_heads[:, None, :]
        decays = jnp.where(same_mask[None], jnp.exp(jnp.where(same_mask[None], gaps_log, 0.0)), 0.0)
        weights = (decays * scores * jnp.transpose(dt_span)[:, None, :]).astype(jnp.bfloat16)
        intra_sum = jnp.einsum('hij,jhp->ihp', weights.astype(jnp.float32), x_span.astype(jnp.float32), precision=lax.Precision.HIGHEST)
        keep_mask = (seg_span == prev_doc).astype(jnp.float32)
        c_heads = jnp.repeat(c_span, repeat_count, axis=1).astype(jnp.float32)
        b_heads = jnp.repeat(b_span, repeat_count, axis=1).astype(jnp.float32)
        carried = jnp.einsum('ihs,hps->ihp', c_heads, carry_state, precision=lax.Precision.HIGHEST)
        carried = carried * (jnp.exp(cum_span) * keep_mask[:, None])[:, :, None]
        span_out = (intra_sum + carried + skip_d[None, :, None] * x_span.astype(jnp.float32)).astype(jnp.bfloat16)
        last_doc = seg_span[span_len - 1]
        tail_weight = jnp.exp(cum_span[span_len - 1][None, :] - cum_span) * dt_span * (seg_span == last_doc).astype(jnp.float32)[:, None]
        fresh_state = jnp.einsum('jhp,jhs->hps', x_span.astype(jnp.float32) * tail_weight[:, :, None], b_heads, precision=lax.Precision.HIGHEST)
        kept = jnp.exp(cum_span[span_len - 1]) * (last_doc == prev_doc).astype(jnp.float32)
        carry_state = carry_state * kept[:, None, None] + fresh_state
        return ((carry_state, last_doc), span_out)
    initial = (jnp.zeros((HEADS, HDIM, STATE), jnp.float32), jnp.array(-1, jnp.int32))
    block_inputs = (x_conv.reshape(span_count, SPAN, HEADS, HDIM), b_all.reshape(span_count, SPAN, GROUPS, STATE), c_all.reshape(span_count, SPAN, GROUPS, STATE), step_size.reshape(span_count, SPAN, HEADS), cum_all, doc_ids.astype(jnp.int32).reshape(span_count, SPAN))
    final_carry, outputs = lax.scan(span_step, initial, block_inputs)
    y_rows = outputs.reshape(TOKENS, inner_width)
    y_float = y_rows.astype(jnp.float32)
    x_float = x_conv.astype(jnp.float32)
    row_sums = jnp.stack([lax.optimization_barrier(jnp.sum(y_float * x_float, axis=1)), lax.optimization_barrier(jnp.sum(y_float * y_float, axis=1)), lax.optimization_barrier(jnp.sum(x_float * x_float, axis=1))], axis=1)
    doc_sums = jax.ops.segment_sum(row_sums, doc_ids.astype(jnp.int32), num_segments=DOCS)
    doc_cosine = doc_sums[:, 0] / jnp.sqrt(doc_sums[:, 1] * doc_sums[:, 2] + 1e-06)
    mixed = gated_norm(y_rows, z_stream, norm_gain, GROUPS)
    return (mixed, doc_cosine)
```

```python
import functools

import jax
import jax.numpy as jnp
from jax import lax
from jax.experimental import pallas as pl
from jax.experimental.pallas import tpu as pltpu
from jax.sharding import PartitionSpec as P

STATE = 256
SPAN = 512
DOCS = 16
CHUNKS = 4
HALO = 16
LANES = 128
VMEM_LIMIT = 20 * 1024 * 1024

F32 = jnp.float32
BF16 = jnp.bfloat16
ANY = pl.BlockSpec(memory_space=pl.ANY)


def iota(shape, dim):
    return lax.broadcasted_iota(jnp.int32, shape, dim)


def whole(shape):
    return pl.BlockSpec(shape, lambda i, pref: (0,) * len(shape))


def call(kernel, rank, inputs, in_specs, out_shapes, out_specs, scratch, name, grid=(1,), cost=None, aliases={}):
    return pl.pallas_call(
        kernel,
        grid_spec=pltpu.PrefetchScalarGridSpec(
            num_scalar_prefetch=1,
            grid=grid,
            in_specs=in_specs,
            out_specs=out_specs,
            scratch_shapes=scratch,
        ),
        out_shape=out_shapes,
        compiler_params=pltpu.CompilerParams(vmem_limit_bytes=VMEM_LIMIT),
        cost_estimate=cost,
        input_output_aliases=aliases,
        name=name,
    )(rank, *inputs)


def cost(us):
    return pl.CostEstimate(flops=int(us * 1e7), bytes_accessed=int(us * 3e4), transcendentals=0)


def pack_kernel(team, chunks, gw, rank_ref, x_ref, bc_ref, dt_ref, *refs):
    xv_ref, tail_ref, bcv_ref, dtv_ref, in_sems, out_sems = refs[-6:]
    outs = list(refs[:-6])
    rank = rank_ref[0]
    rows = x_ref.shape[0]
    cw = gw // chunks
    half = bc_ref.shape[1] // 2

    def fetch(src, dst, sem):
        made = pltpu.make_async_copy(src, dst, in_sems.at[sem])
        made.start()
        return made

    fetches = [fetch(bc_ref, bcv_ref, 0), fetch(dt_ref, dtv_ref, 1)]
    x_fetches = {}
    for k in (2, 3, 1):
        at = pl.multiple_of((rank ^ k) * gw, LANES)
        x_fetches[k] = fetch(x_ref.at[:, pl.ds(at, gw)], xv_ref.at[k - 1], 1 + k)
    tail_fetch = fetch(x_ref.at[pl.ds(rows - HALO, HALO)], tail_ref, 1 + team)

    copies = []

    def copy(src, dst):
        made = pltpu.make_async_copy(src, dst, out_sems.at[len(copies)])
        made.start()
        copies.append(made)

    def copy_bcd(dest, out, first):
        at = pl.multiple_of(dest * STATE, STATE)
        copy(bcv_ref.at[:, pl.ds(at, STATE)], out.at[:, first : first + STATE])
        at = pl.multiple_of(half + dest * STATE, STATE)
        copy(bcv_ref.at[:, pl.ds(at, STATE)], out.at[:, first + STATE : first + 2 * STATE])
        copy(dtv_ref, out.at[:, first + 2 * STATE : first + 2 * STATE + LANES])

    for made in fetches:
        made.wait()
    copy_bcd(rank, outs.pop(0), 0)
    for k in (2, 3):
        copy_bcd(rank ^ k, outs.pop(0), 0)
    near = outs.pop(0)
    copy_bcd(rank ^ 1, near, gw)
    for k in (2, 3):
        x_fetches[k].wait()
        for q in range(chunks):
            copy(xv_ref.at[k - 1, :, pl.ds(q * cw, cw)], outs.pop(0))
    x_fetches[1].wait()
    copy(xv_ref.at[0], near.at[:, 0:gw])
    tail_fetch.wait()
    tail = pl.ds(rows - HALO, HALO)
    for g in range(team):
        out = outs.pop(0)
        copy(tail_ref.at[:, pl.ds(g * gw, gw)], out.at[:, 0:gw])
        copy(bcv_ref.at[tail, pl.ds(g * STATE, STATE)], out.at[:, gw : gw + STATE])
        copy(bcv_ref.at[tail, pl.ds(half + g * STATE, STATE)], out.at[:, gw + STATE : gw + 2 * STATE])
    for made in copies:
        made.wait()


def column_of(row):
    return jnp.transpose(jnp.broadcast_to(row, (LANES, row.shape[1])))


def shift_kernel(taps, rank_ref, docs_ref, shift_ref):
    tiles = shift_ref.shape[0]
    for a in range(tiles):
        near = docs_ref[0:1, a * LANES : (a + 2) * LANES]
        own = column_of(docs_ref[0:1, (a + 1) * LANES : (a + 2) * LANES])
        same = jnp.concatenate([own, own], axis=1) == near
        row, col = iota((LANES, 2 * LANES), 0), iota((LANES, 2 * LANES), 1)
        for back in range(1, taps):
            hit = same & (col == row + (LANES - back))
            shift_ref[a, (back - 1) * LANES : back * LANES, :] = jnp.where(hit, 1.0, 0.0).astype(BF16)


def gather_rows(rank, sources, raw_ref, halo_refs, sems):
    copies = []
    for k, source in enumerate(sources):
        at = pl.multiple_of(LANES + (rank ^ k) * LANES, LANES)
        made = pltpu.make_async_copy(source, raw_ref.at[pl.ds(at, LANES)], sems.at[k])
        made.start()
        copies.append(made)
    halo = halo_refs[0][...].astype(F32)
    for ref in halo_refs[1:]:
        halo = halo + ref[...].astype(F32)
    width = halo.shape[1]
    raw_ref[0 : LANES - HALO, 0:width] = jnp.zeros((LANES - HALO, width), BF16)
    raw_ref[LANES - HALO : LANES, 0:width] = halo.astype(BF16)
    for made in copies:
        made.wait()


def silu(value):
    half = 0.5 * value
    return half + half * jnp.tanh(half)


def conv_tile(raw, shift, taps, bias):
    count = len(taps)
    moved = jnp.dot(shift, raw, preferred_element_type=F32)
    total = raw[LANES:].astype(F32) * taps[count - 1] + bias
    for back in range(1, count):
        total = total + moved[(back - 1) * LANES : back * LANES] * taps[count - 1 - back]
    return silu(total).astype(BF16)


def split_hi(value):
    hi = value.astype(BF16).astype(F32)
    return hi, value - hi


def bc_kernel(team, taps, near_at, rank_ref, *refs):
    bcd = list(refs[:team])
    bcd[1] = bcd[1].at[:, pl.ds(near_at, 2 * STATE + LANES)]
    halo_b = refs[team : 2 * team]
    halo_c = refs[2 * team : 3 * team]
    shift_ref, docs_ref, wb_b_ref, wb_c_ref, heads_ref = refs[3 * team : 3 * team + 5]
    s_ref, bt_ref, cm_ref, uv_ref, row_ref, raw_ref, b_ref, c_ref, sems = refs[3 * team + 5 :]
    rank = rank_ref[0]
    tiles = SPAN // LANES
    own_heads = LANES // team

    copies = []
    for k in range(team):
        at = pl.multiple_of(LANES + (rank ^ k) * LANES, LANES)
        made = pltpu.make_async_copy(bcd[k], raw_ref.at[pl.ds(at, LANES)], sems.at[k])
        made.start()
        copies.append(made)
    raw_ref[0 : LANES - HALO, :] = jnp.zeros((LANES - HALO, raw_ref.shape[1]), BF16)
    for place, parts in ((0, halo_b), (STATE, halo_c)):
        halo = parts[0][...].astype(F32)
        for ref in parts[1:]:
            halo = halo + ref[...].astype(F32)
        raw_ref[LANES - HALO : LANES, place : place + STATE] = halo.astype(BF16)
    for made in copies:
        made.wait()

    lane = iota((LANES, LANES), 1)
    part = lane // own_heads

    def mine(value):
        near = part[: value.shape[0]]
        moved = pltpu.roll(value, (LANES - rank * own_heads) % LANES, 1)
        kept = jnp.where(near == 0, moved, 0.0)
        total = kept
        for step in range(1, team):
            total = total + pltpu.roll(kept, step * own_heads, 1)
        return total

    heads = mine(heads_ref[...])
    bias_row, skip_row = heads[0:1], heads[2:3]
    decay_row = -jnp.exp(heads[1:2])
    ones = jnp.where(iota((LANES, LANES), 0) >= lane, 1.0, 0.0)

    last_doc = docs_ref[0:1, LANES + SPAN - 1 : LANES + SPAN]
    prev_doc = docs_ref[0:1, LANES - 1 : LANES]
    start = jnp.zeros((1, LANES), F32)
    rows_g, rows_e = [], []
    for a in range(tiles):
        here = slice(a * LANES, (a + 1) * LANES)
        raw = raw_ref[a * LANES : (a + 2) * LANES, :]
        shift = shift_ref[a]
        b_tile = conv_tile(raw[:, 0:STATE], shift, [wb_b_ref[i : i + 1, :] for i in range(taps)], wb_b_ref[taps : taps + 1, :])
        c_tile = conv_tile(raw[:, STATE : 2 * STATE], shift, [wb_c_ref[i : i + 1, :] for i in range(taps)], wb_c_ref[taps : taps + 1, :])
        b_ref[here, :] = b_tile
        own = column_of(docs_ref[0:1, (a + 1) * LANES : (a + 2) * LANES])
        own_two = jnp.concatenate([own, own], axis=1)
        cm_ref[here, :] = jnp.where(own_two == prev_doc, c_tile.astype(F32), 0.0).astype(BF16)
        masked = jnp.where(own_two == last_doc, b_tile.astype(F32), 0.0)
        bt_ref[:, here] = jnp.transpose(masked).astype(BF16)
        for b in range(a + 1):
            there = slice(b * LANES, (b + 1) * LANES)
            scores = lax.dot_general(
                c_tile, b_ref[there, :], (((1,), (1,)), ((), ())), preferred_element_type=F32
            )
            keep = own == docs_ref[0:1, (b + 1) * LANES : (b + 2) * LANES]
            if a == b:
                keep = keep & (iota((LANES, LANES), 0) >= lane)
            s_ref[here, there] = jnp.where(keep, scores, 0.0).astype(BF16)
        raised = mine(raw[LANES:, 2 * STATE : 2 * STATE + LANES].astype(F32)) + bias_row
        step = jnp.maximum(raised, 0.0) + jnp.log1p(jnp.exp(-jnp.abs(raised)))
        cum = jnp.dot(ones, decay_row * step, precision=lax.Precision.HIGHEST, preferred_element_type=F32)
        u_hi, u_lo = split_hi(jnp.exp(cum))
        v_hi, v_lo = split_hi(jnp.exp(-cum) * step)
        packed = jnp.where(part == 0, v_hi, jnp.where(part == 1, v_lo, jnp.where(part == 2, u_hi, u_lo)))
        uv_ref[here, :] = packed.astype(BF16)
        tile_total = cum[LANES - 1 : LANES]
        rows_g.append(jnp.exp(tile_total))
        rows_e.append(jnp.exp(start))
        start = start + tile_total
    passes = jnp.exp(start) * jnp.where(last_doc == prev_doc, 1.0, 0.0)
    every = rows_g + rows_e + [skip_row, passes] + [jnp.zeros((1, LANES), F32)] * 6
    hi, lo = split_hi(jnp.concatenate(every, axis=0))
    near = part[: 16]
    row_ref[...] = jnp.where(near == 0, hi, jnp.where(near == 1, lo, 0.0)).astype(BF16)


def spreader(first, width, hdim, own_heads, upper):
    row, col = iota((LANES, width), 0), iota((LANES, width), 1)
    hit = (row % own_heads) == (first + col // hdim)
    half = (row >= 2 * own_heads) if upper else (row < 2 * own_heads)
    return jnp.where(hit & half, 1.0, 0.0).astype(BF16)


def mix_kernel(team, taps, first, hdim, start_col, own_cols, rank_ref, *refs):
    x_ref = refs[0]
    got = refs[1:team]
    halos = refs[team : 2 * team]
    shift_ref, wb_ref, s_ref, bt_ref, uv_ref, row_ref = refs[2 * team : 2 * team + 6]
    xc_ref, yl_ref, st_ref, raw_ref, xf_ref, xb_ref, sems = refs[2 * team + 6 :]
    rank = rank_ref[0]
    tiles = SPAN // LANES
    width = xc_ref.shape[1]
    own_heads = LANES // team
    at = pl.multiple_of(rank * own_cols + start_col, LANES)
    sources = [x_ref.at[:, pl.ds(at, width)], got[0].at[:, pl.ds(start_col, width)], got[1], got[2]]
    gather_rows(rank, sources, raw_ref, halos, sems)
    spread_v = spreader(first, width, hdim, own_heads, False)
    spread_u = spreader(first, width, hdim, own_heads, True)
    rows = jnp.dot(row_ref[...], spread_v, preferred_element_type=F32)
    skip = rows[2 * tiles : 2 * tiles + 1]
    weights = [wb_ref[i : i + 1, :] for i in range(taps)]
    bias = wb_ref[taps : taps + 1, :]
    for a in range(tiles):
        here = slice(a * LANES, (a + 1) * LANES)
        xc = conv_tile(raw_ref[a * LANES : (a + 2) * LANES, :], shift_ref[a], weights, bias)
        xc_ref[here, :] = xc
        xf = xc.astype(F32)
        uv = uv_ref[here, :]
        scaled = jnp.dot(uv, spread_v, preferred_element_type=F32) * xf
        xf_ref[here, :] = scaled
        xb_ref[here, :] = scaled.astype(BF16)
        total = jnp.dot(
            s_ref[here, 0 : (a + 1) * LANES], xb_ref[0 : (a + 1) * LANES, :], preferred_element_type=F32
        )
        yl_ref[here, :] = jnp.dot(uv, spread_u, preferred_element_type=F32) * total + skip * xf
        for b in range(a + 1):
            there = slice(b * LANES, (b + 1) * LANES)
            later = xf_ref[there, :] * rows[a : a + 1]
            if a < tiles - 1:
                xf_ref[there, :] = later
            xb_ref[there, :] = later.astype(BF16)
    st_ref[...] = jnp.dot(bt_ref[...], xb_ref[...], preferred_element_type=F32).astype(BF16)


def carry_kernel(team, first, hdim, rank_ref, st_ref, yl_ref, xc_ref, cm_ref, uv_ref, row_ref, docs_ref, *refs):
    outs = refs[-team - 2 : -2]
    stat_ref, rows_ref = refs[-2:]
    rank = rank_ref[0]
    tiles = SPAN // LANES
    width = xc_ref.shape[1]
    own_heads = LANES // team
    spread_v = spreader(first, width, hdim, own_heads, False)
    spread_u = spreader(first, width, hdim, own_heads, True)
    rows_ref[...] = jnp.dot(row_ref[...], spread_v, preferred_element_type=F32)
    sums = jnp.zeros((DOCS, 3 * LANES), F32)
    for k in range(team):
        tile = rank ^ k
        here = pl.ds(pl.multiple_of(tile * LANES, LANES), LANES)
        came = jnp.dot(cm_ref[here, :], st_ref[...], preferred_element_type=F32)
        decay = jnp.dot(uv_ref[here, :], spread_u, preferred_element_type=F32)
        y = yl_ref[here, :] + decay * (came * rows_ref[pl.ds(tiles + tile, 1), :])
        y = y.astype(BF16)
        outs[k][...] = y
        y = y.astype(F32)
        x = xc_ref[here, :].astype(F32)
        parts = []
        for product in (y * x, y * y, x * x):
            part = product[:, 0:LANES]
            for c in range(1, width // LANES):
                part = part + product[:, c * LANES : (c + 1) * LANES]
            parts.append(part)
        docs = docs_ref[0:1, pl.ds(pl.multiple_of((tile + 1) * LANES, LANES), LANES)]
        table = jnp.where(iota((DOCS, LANES), 0).astype(F32) == docs, 1.0, 0.0)
        sums = sums + jnp.dot(
            table, jnp.concatenate(parts, axis=1), precision=lax.Precision.HIGHEST, preferred_element_type=F32
        )
    lane = iota((DOCS, LANES), 1)
    out = jnp.zeros((DOCS, LANES), F32)
    for i in range(3):
        out = jnp.where(lane == i, jnp.sum(sums[:, i * LANES : (i + 1) * LANES], axis=1, keepdims=True), out)
    stat_ref[...] = out


def norm_kernel(team, chunks, rank_ref, *refs):
    y_refs = refs[:-4]
    z_ref, gain_ref, out_ref, gated_ref = refs[-4:]
    width = z_ref.shape[1]
    cw = width // chunks
    for k in range(team):

        @pl.when(pl.program_id(0) == k)
        def _():
            part = jnp.zeros((LANES, LANES), F32)
            for q in range(chunks):
                cols = slice(q * cw, (q + 1) * cw)
                y = y_refs[k][:, cols] if k < 2 else y_refs[2 + (k - 2) * chunks + q][...]
                gated = y.astype(F32) * silu(z_ref[:, cols].astype(F32))
                gated_ref[:, cols] = gated
                square = gated * gated
                for c in range(cw // LANES):
                    part = part + square[:, c * LANES : (c + 1) * LANES]
            scale = lax.rsqrt(jnp.sum(part, axis=1, keepdims=True) * (1.0 / width) + 1e-05)
            for q in range(chunks):
                cols = slice(q * cw, (q + 1) * cw)
                out_ref[:, cols] = (gated_ref[:, cols] * scale * gain_ref[0:1, cols]).astype(BF16)


def on_device(
    x_stream,
    bc_stream,
    z_stream,
    dt_raw,
    doc_ids,
    conv_weight,
    conv_bias,
    dt_bias,
    a_log,
    skip_d,
    norm_gain,
):
    rows, inner = x_stream.shape
    heads = dt_raw.shape[1]
    hdim = inner // heads
    taps = conv_weight.shape[0]
    members = lax.axis_size("seq")
    team = SPAN // rows
    tiles = SPAN // LANES
    gw = inner // team
    cw = gw // CHUNKS
    me = lax.axis_index("seq")
    rank = jnp.reshape(me % team, (1,)).astype(jnp.int32)
    doc_most = rows * members // 4
    hops = (doc_most - 2) // SPAN + 1

    swap = lambda array, k: lax.ppermute(array, "seq", [(i, i ^ k) for i in range(members)])
    onward = lambda array: lax.ppermute(array, "seq", [(i, i + team) for i in range(members - team)])

    shape = jax.ShapeDtypeStruct
    bcd_w = 2 * STATE + LANES
    halo_w = gw + 2 * STATE
    pack_shapes = (
        [shape((rows, bcd_w), BF16)] * 3
        + [shape((rows, gw + bcd_w), BF16)]
        + [shape((rows, cw), BF16)] * (2 * CHUNKS)
        + [shape((HALO, halo_w), BF16)] * team
    )
    packed = call(
        functools.partial(pack_kernel, team, CHUNKS, gw),
        rank,
        (x_stream, bc_stream, dt_raw),
        [ANY] * 3,
        pack_shapes,
        [ANY] * len(pack_shapes),
        [
            pltpu.VMEM((team - 1, rows, gw), BF16),
            pltpu.VMEM((HALO, inner), BF16),
            pltpu.VMEM(bc_stream.shape, BF16),
            pltpu.VMEM(dt_raw.shape, BF16),
            pltpu.SemaphoreType.DMA((2 + team,)),
            pltpu.SemaphoreType.DMA((3 * team + 2 * CHUNKS + 1 + 3 * team,)),
        ],
        "pack",
        cost=cost(2),
    )
    bcd = [packed[0], None, swap(packed[1], 2), swap(packed[2], 3)]
    bcd[1] = swap(packed[3], 1)
    halos = []
    for g in range(team):
        pairs = [(i, i - i % team + team + g) for i in range(team - 1, members - team, team)]
        halos.append(lax.ppermute(packed[4 + 2 * CHUNKS + g], "seq", pairs))
    got = [
        [bcd[1], swap(packed[4 + q], 2), swap(packed[4 + CHUNKS + q], 3)] for q in range(CHUNKS)
    ]

    ext_docs = jnp.concatenate([jnp.full((LANES,), -1, jnp.int32), doc_ids])
    docs = lax.dynamic_slice_in_dim(ext_docs, (me // team) * SPAN, SPAN + LANES).astype(F32)[None]
    wb = jnp.concatenate([conv_weight, conv_bias[None]], axis=0)
    head_rows = jnp.concatenate(
        [dt_bias[None], a_log[None], skip_d[None], jnp.zeros((5, heads), F32)], axis=0
    )
    shift_shape = (tiles, (taps - 1) * LANES, 2 * LANES)
    shift = call(
        functools.partial(shift_kernel, taps),
        rank,
        (docs,),
        [whole(docs.shape)],
        shape(shift_shape, BF16),
        whole(shift_shape),
        [],
        "shift",
        cost=cost(1.5),
    )

    b_block, c_block = inner // STATE, inner // STATE + team
    scores, b_turned, c_masked, uv, row_pack = call(
        functools.partial(bc_kernel, team, taps, gw),
        rank,
        (*bcd, *halos, *halos, shift, docs, wb, wb, head_rows),
        [ANY] * team
        + [pl.BlockSpec((HALO, STATE), lambda i, pref: (0, gw // STATE))] * team
        + [pl.BlockSpec((HALO, STATE), lambda i, pref: (0, gw // STATE + 1))] * team
        + [
            whole(shift_shape),
            whole(docs.shape),
            pl.BlockSpec((taps + 1, STATE), lambda i, pref: (0, b_block + pref[0])),
            pl.BlockSpec((taps + 1, STATE), lambda i, pref: (0, c_block + pref[0])),
            whole(head_rows.shape),
        ],
        [
            shape((SPAN, SPAN), BF16),
            shape((STATE, SPAN), BF16),
            shape((SPAN, STATE), BF16),
            shape((SPAN, LANES), BF16),
            shape((16, LANES), BF16),
        ],
        [
            whole((SPAN, SPAN)),
            whole((STATE, SPAN)),
            whole((SPAN, STATE)),
            whole((SPAN, LANES)),
            whole((16, LANES)),
        ],
        [
            pltpu.VMEM((LANES + SPAN, bcd_w), BF16),
            pltpu.VMEM((SPAN, STATE), BF16),
            pltpu.VMEM((SPAN, STATE), BF16),
            pltpu.SemaphoreType.DMA((team,)),
        ],
        "bc",
        cost=cost(4),
    )

    per_chunk = cw // hdim
    y_parts, stats = [], None
    for q in range(CHUNKS):
        xc, y_local, fresh = call(
            functools.partial(mix_kernel, team, taps, q * per_chunk, hdim, q * cw, gw),
            rank,
            (x_stream, *got[q], *halos, shift, wb, scores, b_turned, uv, row_pack),
            [ANY] * team
            + [pl.BlockSpec((HALO, cw), lambda i, pref, q=q: (0, q))] * team
            + [
                whole(shift_shape),
                pl.BlockSpec((taps + 1, cw), lambda i, pref, q=q: (0, pref[0] * CHUNKS + q)),
                whole((SPAN, SPAN)),
                whole((STATE, SPAN)),
                whole((SPAN, LANES)),
                whole((16, LANES)),
            ],
            [shape((SPAN, cw), BF16), shape((SPAN, cw), F32), shape((STATE, cw), BF16)],
            [whole((SPAN, cw)), whole((SPAN, cw)), whole((STATE, cw))],
            [
                pltpu.VMEM((LANES + SPAN, cw), BF16),
                pltpu.VMEM((SPAN, cw), F32),
                pltpu.VMEM((SPAN, cw), BF16),
                pltpu.SemaphoreType.DMA((team,)),
            ],
            "mix",
            cost=cost(4),
        )
        state = onward(fresh)
        if hops > 1:
            own_heads = heads // team
            first = q * per_chunk
            part = row_pack[2 * tiles + 1].astype(F32)
            kept = part[first : first + per_chunk] + part[own_heads + first : own_heads + first + per_chunk]
            kept = jnp.repeat(kept, hdim)[None]
            for _ in range(hops - 1):
                state = onward((fresh.astype(F32) + kept * state.astype(F32)).astype(BF16))
        outs = call(
            functools.partial(carry_kernel, team, q * per_chunk, hdim),
            rank,
            (state, y_local, xc, c_masked, uv, row_pack, docs) + ((y_own, y_near) if q else ()),
            [
                whole((STATE, cw)),
                whole((SPAN, cw)),
                whole((SPAN, cw)),
                whole((SPAN, STATE)),
                whole((SPAN, LANES)),
                whole((16, LANES)),
                whole(docs.shape),
            ]
            + [ANY] * (2 if q else 0),
            [shape((rows, gw), BF16)] * 2 + [shape((rows, cw), BF16)] * 2 + [shape((DOCS, LANES), F32)],
            [pl.BlockSpec((rows, cw), lambda i, pref, q=q: (0, q))] * 2
            + [whole((rows, cw))] * 2
            + [whole((DOCS, LANES))],
            [pltpu.VMEM((16, cw), F32)],
            "carry",
            cost=cost(3),
            aliases={8: 0, 9: 1} if q else {},
        )
        y_own, y_near = outs[:2]
        y_parts.append([swap(outs[k], k) for k in (2, 3)])
        stats = outs[team] if stats is None else stats + outs[team]
    y_near = swap(y_near, 1)

    step = 1
    while step < members:
        stats = stats + swap(stats, step)
        step *= 2

    mixed = call(
        functools.partial(norm_kernel, team, CHUNKS),
        rank,
        (y_own, y_near, *[y_parts[q][k] for k in range(2) for q in range(CHUNKS)], z_stream, norm_gain[None]),
        [whole((rows, gw))] * 2
        + [whole((rows, cw))] * (2 * CHUNKS)
        + [
            pl.BlockSpec((rows, gw), lambda i, pref: (0, pref[0] ^ i)),
            pl.BlockSpec((1, gw), lambda i, pref: (0, pref[0] ^ i)),
        ],
        shape((rows, inner), BF16),
        pl.BlockSpec((rows, gw), lambda i, pref: (0, pref[0] ^ i)),
        [pltpu.VMEM((rows, gw), F32)],
        "norm",
        grid=(team,),
        cost=cost(4),
    )
    doc_cosine = stats[:, 0] / jnp.sqrt(stats[:, 1] * stats[:, 2] + 1e-06)
    return (mixed, doc_cosine)


def solution(mesh):
    return jax.shard_map(
        on_device,
        mesh=mesh,
        in_specs=(
            P(("groups", "seq"), None),
            P(("groups", "seq"), None),
            P(("groups", "seq"), None),
            P(("groups", "seq"), None),
            P("groups"),
            P(),
            P(),
            P(),
            P(),
            P(),
            P(),
        ),
        out_specs=(P(("groups", "seq"), None), P("groups")),
        check_vma=False,
    )
```

```python
import functools

import jax
import jax.numpy as jnp
from jax import lax
from jax.experimental import pallas as pl
from jax.experimental.pallas import tpu as pltpu
from jax.sharding import PartitionSpec as P

STATE = 256
SPAN = 512
DOCS = 16
HALO = 16
PARTS = (2, 3, 3)
LANES = 128
VMEM_LIMIT = 20 * 1024 * 1024
VMEM_MOST = 60 * 1024 * 1024

F32 = jnp.float32
BF16 = jnp.bfloat16
ANY = pl.BlockSpec(memory_space=pl.ANY)


def iota(shape, dim):
    return lax.broadcasted_iota(jnp.int32, shape, dim)


def whole(shape):
    return pl.BlockSpec(shape, lambda i, pref: (0,) * len(shape))


def call(kernel, rank, inputs, in_specs, out_shapes, out_specs, scratch, name, grid=(1,), cost=None, aliases={}, limit=VMEM_LIMIT):
    return pl.pallas_call(
        kernel,
        grid_spec=pltpu.PrefetchScalarGridSpec(
            num_scalar_prefetch=1,
            grid=grid,
            in_specs=in_specs,
            out_specs=out_specs,
            scratch_shapes=scratch,
        ),
        out_shape=out_shapes,
        compiler_params=pltpu.CompilerParams(vmem_limit_bytes=limit),
        cost_estimate=cost,
        input_output_aliases=aliases,
        name=name,
    )(rank, *inputs)


def cost(us):
    return pl.CostEstimate(flops=int(us * 1e9), bytes_accessed=int(us * 3e6), transcendentals=0)


def pack_kernel(team, chunks, gw, rank_ref, x_ref, bc_ref, dt_ref, *refs):
    xv_ref, tail_ref, bcv_ref, dtv_ref, in_sems, out_sems = refs[-6:]
    outs = list(refs[:-6])
    rank = rank_ref[0]
    rows = x_ref.shape[0]
    half = bc_ref.shape[1] // 2
    fold = gw * HALO // rows

    def fetch(src, dst, sem):
        made = pltpu.make_async_copy(src, dst, in_sems.at[sem])
        made.start()
        return made

    fetches = [fetch(bc_ref, bcv_ref, 0), fetch(dt_ref, dtv_ref, 1)]
    x_fetches = {}
    for k in (2, 3, 1):
        at = pl.multiple_of((rank ^ k) * gw, LANES)
        x_fetches[k] = fetch(x_ref.at[:, pl.ds(at, gw)], xv_ref.at[k - 1], 1 + k)
    at = pl.multiple_of(rank * gw, LANES)
    last = pl.ds(rows - HALO, HALO)
    tail_fetch = fetch(x_ref.at[last, pl.ds(at, gw)], tail_ref, 1 + team)

    copies = []

    def copy(src, dst):
        made = pltpu.make_async_copy(src, dst, out_sems.at[len(copies)])
        made.start()
        copies.append(made)

    for made in fetches:
        made.wait()
    for k in (2, 3, 1):
        out = outs.pop(0)
        at = pl.multiple_of((rank ^ k) * STATE, STATE)
        copy(bcv_ref.at[:, pl.ds(at, STATE)], out.at[:, 0:STATE])
        at = pl.multiple_of(half + (rank ^ k) * STATE, STATE)
        copy(bcv_ref.at[:, pl.ds(at, STATE)], out.at[:, STATE : 2 * STATE])
        copy(dtv_ref, out.at[:, 2 * STATE : 2 * STATE + LANES])
        x_fetches[k].wait()
        first = 2 * STATE + LANES
        for j in range(rows // HALO):
            tail = xv_ref.at[k - 1, pl.ds(rows - HALO, HALO), pl.ds(j * fold, fold)]
            copy(tail, out.at[pl.ds(j * HALO, HALO), first : first + fold])
        size = gw if k == 1 else chunks[0]
        copy(xv_ref.at[k - 1, :, pl.ds(0, size)], out.at[:, first + fold : first + fold + size])
    done = chunks[0]
    for size in chunks[1:]:
        for k in (2, 3):
            copy(xv_ref.at[k - 1, :, pl.ds(done, size)], outs.pop(0))
        done += size
    out = outs.pop(0)
    b_at = pl.multiple_of(rank * STATE, LANES)
    c_at = pl.multiple_of(half + rank * STATE, LANES)
    copy(bcv_ref.at[last, pl.ds(b_at, STATE)], out.at[:, gw : gw + STATE])
    copy(bcv_ref.at[last, pl.ds(c_at, STATE)], out.at[:, gw + STATE : gw + 2 * STATE])
    tail_fetch.wait()
    copy(tail_ref, out.at[:, 0:gw])
    for made in copies:
        made.wait()


def relay_kernel(team, gw, rank_ref, tail_ref, *refs):
    got = refs[: team - 1]
    out_ref, sems = refs[team - 1 :]
    rank = rank_ref[0]
    rows = got[0].shape[0]
    fold = gw * HALO // rows
    tail = pl.ds(rows - HALO, HALO)

    def copy_all(pairs):
        copies = []
        for i, (src, dst) in enumerate(pairs):
            made = pltpu.make_async_copy(src, dst, sems.at[i])
            made.start()
            copies.append(made)
        for made in copies:
            made.wait()

    @pl.when(rank == team - 1)
    def _():
        out_ref[...] = tail_ref[...]

    for k in range(1, team):

        @pl.when(rank ^ k == team - 1)
        def _():
            first = 2 * STATE + LANES
            pairs = [(got[k - 1].at[tail, 0 : 2 * STATE], out_ref.at[:, gw : gw + 2 * STATE])]
            for j in range(rows // HALO):
                src = got[k - 1].at[pl.ds(j * HALO, HALO), first : first + fold]
                pairs.append((src, out_ref.at[:, j * fold : (j + 1) * fold]))
            copy_all(pairs)


def column_of(row):
    return jnp.transpose(jnp.broadcast_to(row, (LANES, row.shape[1])))


def shift_kernel(taps, rank_ref, docs_ref, shift_ref):
    tiles = shift_ref.shape[0]
    for a in range(tiles):
        near = docs_ref[0:1, a * LANES : (a + 2) * LANES]
        own = column_of(docs_ref[0:1, (a + 1) * LANES : (a + 2) * LANES])
        same = jnp.concatenate([own, own], axis=1) == near
        row, col = iota((LANES, 2 * LANES), 0), iota((LANES, 2 * LANES), 1)
        for back in range(1, taps):
            hit = same & (col == row + (LANES - back))
            shift_ref[a, (back - 1) * LANES : back * LANES, :] = jnp.where(hit, 1.0, 0.0).astype(BF16)


def gather_rows(rank, sources, raw_ref, halo, sems):
    copies = []
    for k, parts in enumerate(sources):
        at = pl.multiple_of(LANES + (rank ^ k) * LANES, LANES)
        for source, first in parts:
            dst = raw_ref.at[pl.ds(at, LANES), first : first + source.shape[1]]
            made = pltpu.make_async_copy(source, dst, sems.at[len(copies)])
            made.start()
            copies.append(made)
    width = halo.shape[1]
    raw_ref[0 : LANES - HALO, 0:width] = jnp.zeros((LANES - HALO, width), BF16)
    raw_ref[LANES - HALO : LANES, 0:width] = halo
    for made in copies:
        made.wait()


def silu(value):
    half = 0.5 * value
    return half + half * jnp.tanh(half)


def conv_tile(raw, shift, taps, bias):
    count = len(taps)
    moved = jnp.dot(shift, raw, preferred_element_type=F32)
    total = raw[LANES:].astype(F32) * taps[count - 1] + bias
    for back in range(1, count):
        total = total + moved[(back - 1) * LANES : back * LANES] * taps[count - 1 - back]
    return silu(total).astype(BF16)


def split_hi(value):
    hi = value.astype(BF16).astype(F32)
    return hi, value - hi


def bc_kernel(team, taps, gw, rank_ref, bc_ref, dt_ref, *refs):
    got = refs[: team - 1]
    halo_ref, shift_ref, docs_ref, wb_b_ref, wb_c_ref, heads_ref = refs[team - 1 : team + 5]
    s_ref, bt_ref, cm_ref, uv_ref, row_ref, raw_ref, b_ref, sems = refs[team + 5 :]
    rank = rank_ref[0]
    tiles = SPAN // LANES
    own_heads = LANES // team
    half = bc_ref.shape[1] // 2
    b_at = pl.multiple_of(rank * STATE, LANES)
    c_at = pl.multiple_of(half + rank * STATE, LANES)
    own = [(bc_ref.at[:, pl.ds(b_at, STATE)], 0), (bc_ref.at[:, pl.ds(c_at, STATE)], STATE), (dt_ref, 2 * STATE)]
    others = [[(ref.at[:, 0 : 2 * STATE + LANES], 0)] for ref in got]
    gather_rows(rank, [own] + others, raw_ref, halo_ref[:, gw : gw + 2 * STATE], sems)

    lane = iota((LANES, LANES), 1)
    part = lane // own_heads

    def mine(value):
        near = part[: value.shape[0]]
        moved = pltpu.roll(value, (LANES - rank * own_heads) % LANES, 1)
        kept = jnp.where(near == 0, moved, 0.0)
        total = kept
        for step in range(1, team):
            total = total + pltpu.roll(kept, step * own_heads, 1)
        return total

    heads = mine(heads_ref[...])
    bias_row, skip_row = heads[0:1], heads[2:3]
    decay_row = -jnp.exp(heads[1:2])
    ones = jnp.where(iota((LANES, LANES), 0) >= lane, 1.0, 0.0)

    last_doc = docs_ref[0:1, LANES + SPAN - 1 : LANES + SPAN]
    prev_doc = docs_ref[0:1, LANES - 1 : LANES]
    start = jnp.zeros((1, LANES), F32)
    rows_g, rows_e = [], []
    for a in range(tiles):
        here = slice(a * LANES, (a + 1) * LANES)
        raw = raw_ref[a * LANES : (a + 2) * LANES, :]
        shift = shift_ref[a]
        b_tile = conv_tile(raw[:, 0:STATE], shift, [wb_b_ref[i : i + 1, :] for i in range(taps)], wb_b_ref[taps : taps + 1, :])
        c_tile = conv_tile(raw[:, STATE : 2 * STATE], shift, [wb_c_ref[i : i + 1, :] for i in range(taps)], wb_c_ref[taps : taps + 1, :])
        b_ref[here, :] = b_tile
        own = column_of(docs_ref[0:1, (a + 1) * LANES : (a + 2) * LANES])
        own_two = jnp.concatenate([own, own], axis=1)
        cm_ref[here, :] = jnp.where(own_two == prev_doc, c_tile.astype(F32), 0.0).astype(BF16)
        masked = jnp.where(own_two == last_doc, b_tile.astype(F32), 0.0)
        bt_ref[:, here] = jnp.transpose(masked).astype(BF16)
        for b in range(a + 1):
            there = slice(b * LANES, (b + 1) * LANES)
            scores = lax.dot_general(
                c_tile, b_ref[there, :], (((1,), (1,)), ((), ())), preferred_element_type=F32
            )
            keep = own == docs_ref[0:1, (b + 1) * LANES : (b + 2) * LANES]
            if a == b:
                keep = keep & (iota((LANES, LANES), 0) >= lane)
            s_ref[here, there] = jnp.where(keep, scores, 0.0).astype(BF16)
        raised = mine(raw[LANES:, 2 * STATE : 2 * STATE + LANES].astype(F32)) + bias_row
        step = jnp.maximum(raised, 0.0) + jnp.log1p(jnp.exp(-jnp.abs(raised)))
        cum = jnp.dot(ones, decay_row * step, precision=lax.Precision.HIGHEST, preferred_element_type=F32)
        u_hi, u_lo = split_hi(jnp.exp(cum))
        v_hi, v_lo = split_hi(jnp.exp(-cum) * step)
        packed = jnp.where(part == 0, v_hi, jnp.where(part == 1, v_lo, jnp.where(part == 2, u_hi, u_lo)))
        uv_ref[here, :] = packed.astype(BF16)
        tile_total = cum[LANES - 1 : LANES]
        rows_g.append(jnp.exp(tile_total))
        rows_e.append(jnp.exp(start))
        start = start + tile_total
    passes = jnp.exp(start) * jnp.where(last_doc == prev_doc, 1.0, 0.0)
    every = rows_g + rows_e + [skip_row, passes] + [jnp.zeros((1, LANES), F32)] * 6
    hi, lo = split_hi(jnp.concatenate(every, axis=0))
    near = part[: 16]
    row_ref[...] = jnp.where(near == 0, hi, jnp.where(near == 1, lo, 0.0)).astype(BF16)


def spreader(first, width, hdim, own_heads, upper):
    row, col = iota((LANES, width), 0), iota((LANES, width), 1)
    hit = (row % own_heads) == (first + col // hdim)
    half = (row >= 2 * own_heads) if upper else (row < 2 * own_heads)
    return jnp.where(hit & half, 1.0, 0.0).astype(BF16)


def mix_kernel(team, taps, hdim, gw, start, places, rank_ref, *refs):
    x_ref = refs[0]
    got = refs[1:team]
    halo_ref, shift_ref, wb_ref, s_ref, bt_ref, uv_ref, row_ref = refs[team : team + 7]
    xc_ref, yl_ref, st_ref, raw_ref, xf_ref, xb_ref, sems = refs[-7:]
    rank = rank_ref[0]
    tiles = SPAN // LANES
    width = xc_ref.shape[1]
    own_heads = LANES // team
    first = start // hdim
    cols = slice(start, start + width)
    at = pl.multiple_of(rank * gw + start, LANES)
    sources = [[(x_ref.at[:, pl.ds(at, width)], 0)]]
    for ref, place in zip(got, places):
        sources.append([(ref.at[:, place : place + width], 0)])
    gather_rows(rank, sources, raw_ref, halo_ref[:, cols], sems)
    spread_v = spreader(first, width, hdim, own_heads, False)
    spread_u = spreader(first, width, hdim, own_heads, True)
    rows = jnp.dot(row_ref[...], spread_v, preferred_element_type=F32)
    skip = rows[2 * tiles : 2 * tiles + 1]
    weights = [wb_ref[i : i + 1, cols] for i in range(taps)]
    bias = wb_ref[taps : taps + 1, cols]
    for a in range(tiles):
        here = slice(a * LANES, (a + 1) * LANES)
        xc = conv_tile(raw_ref[a * LANES : (a + 2) * LANES, :], shift_ref[a], weights, bias)
        xc_ref[here, :] = xc
        xf = xc.astype(F32)
        uv = uv_ref[here, :]
        scaled = jnp.dot(uv, spread_v, preferred_element_type=F32) * xf
        xf_ref[here, :] = scaled
        xb_ref[here, :] = scaled.astype(BF16)
        total = jnp.dot(
            s_ref[here, 0 : (a + 1) * LANES], xb_ref[0 : (a + 1) * LANES, :], preferred_element_type=F32
        )
        yl_ref[here, :] = jnp.dot(uv, spread_u, preferred_element_type=F32) * total + skip * xf
        for b in range(a + 1):
            there = slice(b * LANES, (b + 1) * LANES)
            later = xf_ref[there, :] * rows[a : a + 1]
            if a < tiles - 1:
                xf_ref[there, :] = later
            xb_ref[there, :] = later.astype(BF16)
    st_ref[...] = jnp.dot(bt_ref[...], xb_ref[...], preferred_element_type=F32).astype(BF16)


def carry_kernel(team, start, hdim, rank_ref, st_ref, yl_ref, xc_ref, cm_ref, uv_ref, row_ref, docs_ref, *refs):
    own_ref, near_ref, far_ref, across_ref, stat_ref, rows_ref, held_ref, sem = refs[-8:]
    first = start // hdim
    rank = rank_ref[0]
    tiles = SPAN // LANES
    width = xc_ref.shape[1]
    own_heads = LANES // team
    spread_v = spreader(first, width, hdim, own_heads, False)
    spread_u = spreader(first, width, hdim, own_heads, True)
    rows_ref[...] = jnp.dot(row_ref[...], spread_v, preferred_element_type=F32)
    sums = jnp.zeros((DOCS, 3 * LANES), F32)
    for k in (1, 2, 3, 0):
        tile = rank ^ k
        here = pl.ds(pl.multiple_of(tile * LANES, LANES), LANES)
        came = jnp.dot(cm_ref[here, :], st_ref[...], preferred_element_type=F32)
        decay = jnp.dot(uv_ref[here, :], spread_u, preferred_element_type=F32)
        y = yl_ref[here, :] + decay * (came * rows_ref[pl.ds(tiles + tile, 1), :])
        y = y.astype(BF16)
        if k == 1:
            held_ref[...] = y
            near = pltpu.make_async_copy(held_ref, near_ref.at[:, start : start + width], sem)
            near.start()
        else:
            (own_ref, None, far_ref, across_ref)[k][...] = y
        y = y.astype(F32)
        x = xc_ref[here, :].astype(F32)
        parts = []
        for product in (y * x, y * y, x * x):
            part = product[:, 0:LANES]
            for c in range(1, width // LANES):
                part = part + product[:, c * LANES : (c + 1) * LANES]
            parts.append(part)
        docs = docs_ref[0:1, pl.ds(pl.multiple_of((tile + 1) * LANES, LANES), LANES)]
        table = jnp.where(iota((DOCS, LANES), 0).astype(F32) == docs, 1.0, 0.0)
        sums = sums + jnp.dot(
            table, jnp.concatenate(parts, axis=1), precision=lax.Precision.HIGHEST, preferred_element_type=F32
        )
    lane = iota((DOCS, LANES), 1)
    out = jnp.zeros((DOCS, LANES), F32)
    for i in range(3):
        out = jnp.where(lane == i, jnp.sum(sums[:, i * LANES : (i + 1) * LANES], axis=1, keepdims=True), out)
    stat_ref[...] = out
    near.wait()


def sum_kernel(rank_ref, *refs):
    total = refs[0][...]
    for ref in refs[1:-1]:
        total = total + ref[...]
    refs[-1][...] = total


def norm_kernel(blocks, rank_ref, *refs):
    y_count = sum(len(block) for block in blocks)
    z_ref, gain_ref = refs[y_count : y_count + 2]
    out_ref, gated_ref = refs[-2:]
    width = z_ref.shape[1]
    for step, block in enumerate(blocks):

        @pl.when(pl.program_id(0) == step)
        def _():
            part = jnp.zeros((LANES, LANES), F32)
            done = 0
            for at in block:
                y_ref = refs[at]
                size = y_ref.shape[1]
                cols = slice(done, done + size)
                gated = y_ref[...].astype(F32) * silu(z_ref[:, cols].astype(F32))
                gated_ref[:, cols] = gated
                square = gated * gated
                for c in range(size // LANES):
                    part = part + square[:, c * LANES : (c + 1) * LANES]
                done += size
            scale = lax.rsqrt(jnp.sum(part, axis=1, keepdims=True) * (1.0 / width) + 1e-05)
            for c in range(width // (4 * LANES)):
                cols = slice(c * 4 * LANES, (c + 1) * 4 * LANES)
                out_ref[:, cols] = (gated_ref[:, cols] * scale * gain_ref[0:1, cols]).astype(BF16)


def on_device(
    x_stream,
    bc_stream,
    z_stream,
    dt_raw,
    doc_ids,
    conv_weight,
    conv_bias,
    dt_bias,
    a_log,
    skip_d,
    norm_gain,
):
    rows, inner = x_stream.shape
    heads = dt_raw.shape[1]
    hdim = inner // heads
    taps = conv_weight.shape[0]
    members = lax.axis_size("seq")
    team = SPAN // rows
    tiles = SPAN // LANES
    gw = inner // team
    chunks = [gw // 8 * part for part in PARTS]
    me = lax.axis_index("seq")
    rank = jnp.reshape(me % team, (1,)).astype(jnp.int32)
    doc_most = rows * members // 4
    hops = (doc_most - 2) // SPAN + 1

    def swap(array, k):
        return lax.ppermute(array, "seq", [(i, i ^ k) for i in range(members)])

    def onward(array):
        return lax.ppermute(array, "seq", [(i, i + team) for i in range(members - team)])

    shape = jax.ShapeDtypeStruct
    bcd_w = 2 * STATE + LANES
    lead_w = bcd_w + gw * HALO // rows
    widths = [lead_w + chunks[0]] * 2 + [lead_w + gw] + [size for size in chunks[1:] for _ in range(2)]
    halo_shape = (HALO, gw + 2 * STATE)
    packed = call(
        functools.partial(pack_kernel, team, chunks, gw),
        rank,
        (x_stream, bc_stream, dt_raw),
        [ANY] * 3,
        [shape((rows, width), BF16) for width in widths] + [shape(halo_shape, BF16)],
        [ANY] * (len(widths) + 1),
        [
            pltpu.VMEM((team - 1, rows, gw), BF16),
            pltpu.VMEM((HALO, gw), BF16),
            pltpu.VMEM(bc_stream.shape, BF16),
            pltpu.VMEM(dt_raw.shape, BF16),
            pltpu.SemaphoreType.DMA((2 + team,)),
            pltpu.SemaphoreType.DMA((3 * (4 + rows // HALO) + 2 * len(chunks) + 3,)),
        ],
        "pack",
        cost=cost(2),
        limit=VMEM_MOST,
    )
    near = swap(packed[2], 1)
    lead = [near, swap(packed[0], 2), swap(packed[1], 3)]
    got = [lead]
    for q in range(1, len(chunks)):
        got.append([near, swap(packed[1 + 2 * q], 2), swap(packed[2 + 2 * q], 3)])

    ext_docs = jnp.concatenate([jnp.full((LANES,), -1, jnp.int32), doc_ids])
    docs = lax.dynamic_slice_in_dim(ext_docs, (me // team) * SPAN, SPAN + LANES).astype(F32)[None]
    wb = jnp.concatenate([conv_weight, conv_bias[None]], axis=0)
    head_rows = jnp.concatenate(
        [dt_bias[None], a_log[None], skip_d[None], jnp.zeros((5, heads), F32)], axis=0
    )
    shift_shape = (tiles, (taps - 1) * LANES, 2 * LANES)
    shift = call(
        functools.partial(shift_kernel, taps),
        rank,
        (docs,),
        [whole(docs.shape)],
        shape(shift_shape, BF16),
        whole(shift_shape),
        [],
        "shift",
        cost=cost(1.5),
    )
    halo = onward(
        call(
            functools.partial(relay_kernel, team, gw),
            rank,
            (packed[-1], *lead),
            [whole(halo_shape)] + [ANY] * (team - 1),
            shape(halo_shape, BF16),
            whole(halo_shape),
            [pltpu.SemaphoreType.DMA((1 + rows // HALO,))],
            "relay",
            cost=cost(1),
        )
    )

    b_block, c_block = inner // STATE, inner // STATE + team
    scores, b_turned, c_masked, uv, row_pack = call(
        functools.partial(bc_kernel, team, taps, gw),
        rank,
        (bc_stream, dt_raw, *lead, halo, shift, docs, wb, wb, head_rows),
        [ANY] * 2
        + [ANY] * (team - 1)
        + [
            whole(halo_shape),
            whole(shift_shape),
            whole(docs.shape),
            pl.BlockSpec((taps + 1, STATE), lambda i, pref: (0, b_block + pref[0])),
            pl.BlockSpec((taps + 1, STATE), lambda i, pref: (0, c_block + pref[0])),
            whole(head_rows.shape),
        ],
        [
            shape((SPAN, SPAN), BF16),
            shape((STATE, SPAN), BF16),
            shape((SPAN, STATE), BF16),
            shape((SPAN, LANES), BF16),
            shape((16, LANES), BF16),
        ],
        [
            whole((SPAN, SPAN)),
            whole((STATE, SPAN)),
            whole((SPAN, STATE)),
            whole((SPAN, LANES)),
            whole((16, LANES)),
        ],
        [
            pltpu.VMEM((LANES + SPAN, bcd_w), BF16),
            pltpu.VMEM((SPAN, STATE), BF16),
            pltpu.SemaphoreType.DMA((team + 2,)),
        ],
        "bc",
        cost=cost(4),
    )

    def mix(q, after):
        start, size = sum(chunks[:q]), chunks[q]
        far = lead_w if q == 0 else 0
        xc, y_local, fresh = call(
            functools.partial(mix_kernel, team, taps, hdim, gw, start, (lead_w + start, far, far)),
            rank,
            (x_stream, *got[q], halo, shift, wb, scores, b_turned, uv, row_pack, *after),
            [ANY]
            + [ANY] * (team - 1)
            + [
                whole(halo_shape),
                whole(shift_shape),
                pl.BlockSpec((taps + 1, gw), lambda i, pref: (0, pref[0])),
                whole((SPAN, SPAN)),
                whole((STATE, SPAN)),
                whole((SPAN, LANES)),
                whole((16, LANES)),
            ]
            + [ANY] * len(after),
            [shape((SPAN, size), BF16), shape((SPAN, size), F32), shape((STATE, size), BF16)],
            [whole((SPAN, size)), whole((SPAN, size)), whole((STATE, size))],
            [
                pltpu.VMEM((LANES + SPAN, size), BF16),
                pltpu.VMEM((SPAN, size), F32),
                pltpu.VMEM((SPAN, size), BF16),
                pltpu.SemaphoreType.DMA((team,)),
            ],
            "mix",
            cost=cost(4),
        )
        state = onward(fresh)
        if hops > 1:
            first, count, own_heads = start // hdim, size // hdim, heads // team
            part = row_pack[2 * tiles + 1].astype(F32)
            kept = part[first : first + count] + part[own_heads + first : own_heads + first + count]
            kept = jnp.repeat(kept, hdim)[None]
            for _ in range(hops - 1):
                state = onward((fresh.astype(F32) + kept * state.astype(F32)).astype(BF16))
        return state, y_local, xc

    def carry(q, mixed, y_near, after):
        start, size = sum(chunks[:q]), chunks[q]
        before = [y_near] if q else []
        return call(
            functools.partial(carry_kernel, team, start, hdim),
            rank,
            (*mixed, c_masked, uv, row_pack, docs, *before, *after),
            [
                whole((STATE, size)),
                whole((SPAN, size)),
                whole((SPAN, size)),
                whole((SPAN, STATE)),
                whole((SPAN, LANES)),
                whole((16, LANES)),
                whole(docs.shape),
            ]
            + [ANY] * (len(before) + len(after)),
            [shape((rows, size), BF16), shape((rows, gw), BF16)]
            + [shape((rows, size), BF16)] * 2
            + [shape((DOCS, LANES), F32)],
            [whole((rows, size)), ANY, whole((rows, size)), whole((rows, size)), whole((DOCS, LANES))],
            [pltpu.VMEM((16, size), F32), pltpu.VMEM((rows, size), BF16), pltpu.SemaphoreType.DMA],
            "carry",
            cost=cost(3),
            aliases={8: 1} if q else {},
        )

    y_own, y_far, y_across, stats, y_near = [], [], [], [], None
    ready = [mix(0, []), mix(1, [])]
    for q in range(len(chunks)):
        after = [y_far[q - 1], y_across[q - 1]] if q else []
        own, y_near, far, across, sums = carry(q, ready[q], y_near, after)
        y_own.append(own)
        y_far.append(swap(far, 2))
        y_across.append(swap(across, 3))
        stats.append(sums)
        if q + 2 < len(chunks):
            ready.append(mix(q + 2, [sums]))
    y_near = swap(y_near, 1)

    stats = call(
        sum_kernel,
        rank,
        tuple(stats),
        [whole((DOCS, LANES))] * len(stats),
        shape((DOCS, LANES), F32),
        whole((DOCS, LANES)),
        [],
        "sums",
        cost=cost(0.1),
    )
    step = 1
    while step < members:
        stats = stats + swap(stats, step)
        step *= 2

    gain = norm_gain[None]

    def norm(blocks, first, before):
        parts = [array for block in blocks for array in block]
        places, done = [], 0
        for block in blocks:
            places.append(list(range(done, done + len(block))))
            done += len(block)
        place = pl.BlockSpec((rows, gw), lambda i, pref: (0, pref[0] ^ (first + i)))
        return call(
            functools.partial(norm_kernel, places),
            rank,
            (*parts, z_stream, gain, *before),
            [whole(array.shape) for array in parts]
            + [place, pl.BlockSpec((1, gw), lambda i, pref: (0, pref[0] ^ (first + i)))]
            + [ANY] * len(before),
            shape((rows, inner), BF16),
            place,
            [pltpu.VMEM((rows, gw), F32)],
            "norm",
            grid=(len(blocks),),
            cost=cost(0.2),
            aliases={len(parts) + 3: 0} if before else {},
        )

    mixed = norm([y_own, [y_near]], 0, [])
    mixed = norm([y_far, y_across], 2, [mixed])
    doc_cosine = stats[:, 0] / jnp.sqrt(stats[:, 1] * stats[:, 2] + 1e-06)
    return (mixed, doc_cosine)


def solution(mesh):
    return jax.shard_map(
        on_device,
        mesh=mesh,
        in_specs=(
            P(("groups", "seq"), None),
            P(("groups", "seq"), None),
            P(("groups", "seq"), None),
            P(("groups", "seq"), None),
            P("groups"),
            P(),
            P(),
            P(),
            P(),
            P(),
            P(),
        ),
        out_specs=(P(("groups", "seq"), None), P("groups")),
        check_vma=False,
    )
```

```python
import functools

import jax
import jax.numpy as jnp
from jax import lax
from jax.experimental import pallas as pl
from jax.experimental.pallas import tpu as pltpu
from jax.sharding import PartitionSpec as P

STATE = 256
SPAN = 512
DOCS = 16
HALO = 16
PARTS = (2, 3, 3)
LANES = 128
VMEM_LIMIT = 20 * 1024 * 1024
VMEM_MOST = 60 * 1024 * 1024

F32 = jnp.float32
BF16 = jnp.bfloat16
ANY = pl.BlockSpec(memory_space=pl.ANY)


def iota(shape, dim):
    return lax.broadcasted_iota(jnp.int32, shape, dim)


def whole(shape):
    return pl.BlockSpec(shape, lambda i, pref: (0,) * len(shape))


def call(kernel, rank, inputs, in_specs, out_shapes, out_specs, scratch, name, grid=(1,), cost=None, aliases={}, limit=VMEM_LIMIT):
    return pl.pallas_call(
        kernel,
        grid_spec=pltpu.PrefetchScalarGridSpec(
            num_scalar_prefetch=1,
            grid=grid,
            in_specs=in_specs,
            out_specs=out_specs,
            scratch_shapes=scratch,
        ),
        out_shape=out_shapes,
        compiler_params=pltpu.CompilerParams(vmem_limit_bytes=limit),
        cost_estimate=cost,
        input_output_aliases=aliases,
        name=name,
    )(rank, *inputs)


def cost(us):
    return pl.CostEstimate(flops=int(us * 1e9), bytes_accessed=int(us * 3e6), transcendentals=0)


def pack_kernel(team, gw, rank_ref, x_ref, bc_ref, dt_ref, *refs):
    xv_ref, tail_ref, bcv_ref, dtv_ref, in_sems, out_sems = refs[-6:]
    outs = list(refs[:-6])
    rank = rank_ref[0]
    rows = x_ref.shape[0]
    half = bc_ref.shape[1] // 2
    fold = gw * HALO // rows
    last = pl.ds(rows - HALO, HALO)

    def fetch(src, dst, sem):
        made = pltpu.make_async_copy(src, dst, in_sems.at[sem])
        made.start()
        return made

    fetches = [
        fetch(bc_ref, bcv_ref, 0),
        fetch(dt_ref, dtv_ref, 1),
        fetch(x_ref.at[last], tail_ref, 2),
        fetch(x_ref.at[:, pl.ds(pl.multiple_of((rank ^ 1) * gw, LANES), gw)], xv_ref, 3),
    ]
    copies = []

    def copy(src, dst):
        made = pltpu.make_async_copy(src, dst, out_sems.at[len(copies)])
        made.start()
        copies.append(made)

    for made in fetches[:3]:
        made.wait()
    def copy_tail(dest, out):
        at = pl.multiple_of(dest * gw, LANES)
        b_at = pl.multiple_of(dest * STATE, LANES)
        c_at = pl.multiple_of(half + dest * STATE, LANES)
        copy(tail_ref.at[:, pl.ds(at, gw)], out.at[:, 0:gw])
        copy(bcv_ref.at[last, pl.ds(b_at, STATE)], out.at[:, gw : gw + STATE])
        copy(bcv_ref.at[last, pl.ds(c_at, STATE)], out.at[:, gw + STATE : gw + 2 * STATE])

    for k in (2, 3, 1):
        out = outs.pop(0)
        at = pl.multiple_of((rank ^ k) * STATE, STATE)
        copy(bcv_ref.at[:, pl.ds(at, STATE)], out.at[:, 0:STATE])
        at = pl.multiple_of(half + (rank ^ k) * STATE, STATE)
        copy(bcv_ref.at[:, pl.ds(at, STATE)], out.at[:, STATE : 2 * STATE])
        copy(dtv_ref, out.at[:, 2 * STATE : 2 * STATE + LANES])
    first = 2 * STATE + LANES
    for j in range(rows // HALO):
        at = pl.multiple_of((rank ^ 1) * gw + j * fold, LANES)
        copy(tail_ref.at[:, pl.ds(at, fold)], out.at[pl.ds(j * HALO, HALO), first : first + fold])
    fetches[3].wait()
    copy(xv_ref, out.at[:, first + fold : first + fold + gw])
    for k in (2, 3, 0):
        copy_tail(rank ^ k, outs.pop(0))
    for made in copies:
        made.wait()


def chunk_kernel(chunks, gw, rank_ref, x_ref, after_ref, *refs):
    xv_ref, in_sems, out_sems = refs[-3:]
    outs = list(refs[:-3])
    rank = rank_ref[0]
    fetches, copies = [], []
    for i, k in enumerate((2, 3)):
        at = pl.multiple_of((rank ^ k) * gw, LANES)
        made = pltpu.make_async_copy(x_ref.at[:, pl.ds(at, gw)], xv_ref.at[i], in_sems.at[i])
        made.start()
        fetches.append(made)
    for made in fetches:
        made.wait()
    done = 0
    for size in chunks:
        for i in range(2):
            src = xv_ref.at[i, :, pl.ds(done, size)]
            made = pltpu.make_async_copy(src, outs.pop(0), out_sems.at[len(copies)])
            made.start()
            copies.append(made)
        done += size
    for made in copies:
        made.wait()


def relay_kernel(team, gw, rank_ref, tail_ref, near_ref, *refs):
    others = {0: tail_ref, 2: refs[0], 3: refs[1]}
    out_ref, sems = refs[-2:]
    rank = rank_ref[0]
    rows = near_ref.shape[0]
    fold = gw * HALO // rows
    tail = pl.ds(rows - HALO, HALO)

    def copy_all(pairs):
        copies = []
        for i, (src, dst) in enumerate(pairs):
            made = pltpu.make_async_copy(src, dst, sems.at[i])
            made.start()
            copies.append(made)
        for made in copies:
            made.wait()

    for k, ref in others.items():

        @pl.when(rank ^ k == team - 1)
        def _():
            copy_all([(ref, out_ref)])

    @pl.when(rank ^ 1 == team - 1)
    def _():
        first = 2 * STATE + LANES
        pairs = [(near_ref.at[tail, 0 : 2 * STATE], out_ref.at[:, gw : gw + 2 * STATE])]
        for j in range(rows // HALO):
            src = near_ref.at[pl.ds(j * HALO, HALO), first : first + fold]
            pairs.append((src, out_ref.at[:, j * fold : (j + 1) * fold]))
        copy_all(pairs)


def column_of(row):
    return jnp.transpose(jnp.broadcast_to(row, (LANES, row.shape[1])))


def shift_kernel(taps, rank_ref, docs_ref, shift_ref):
    tiles = shift_ref.shape[0]
    for a in range(tiles):
        near = docs_ref[0:1, a * LANES : (a + 2) * LANES]
        own = column_of(docs_ref[0:1, (a + 1) * LANES : (a + 2) * LANES])
        same = jnp.concatenate([own, own], axis=1) == near
        row, col = iota((LANES, 2 * LANES), 0), iota((LANES, 2 * LANES), 1)
        for back in range(1, taps):
            hit = same & (col == row + (LANES - back))
            shift_ref[a, (back - 1) * LANES : back * LANES, :] = jnp.where(hit, 1.0, 0.0).astype(BF16)


def gather_rows(rank, sources, raw_ref, halo, sems):
    copies = []
    for k, parts in enumerate(sources):
        at = pl.multiple_of(LANES + (rank ^ k) * LANES, LANES)
        for source, first in parts:
            dst = raw_ref.at[pl.ds(at, LANES), first : first + source.shape[1]]
            made = pltpu.make_async_copy(source, dst, sems.at[len(copies)])
            made.start()
            copies.append(made)
    width = halo.shape[1]
    raw_ref[0 : LANES - HALO, 0:width] = jnp.zeros((LANES - HALO, width), BF16)
    raw_ref[LANES - HALO : LANES, 0:width] = halo
    for made in copies:
        made.wait()


def silu(value):
    half = 0.5 * value
    return half + half * jnp.tanh(half)


def conv_tile(raw, shift, taps, bias):
    count = len(taps)
    moved = jnp.dot(shift, raw, preferred_element_type=F32)
    total = raw[LANES:].astype(F32) * taps[count - 1] + bias
    for back in range(1, count):
        total = total + moved[(back - 1) * LANES : back * LANES] * taps[count - 1 - back]
    return silu(total).astype(BF16)


def split_hi(value):
    hi = value.astype(BF16).astype(F32)
    return hi, value - hi


def bc_kernel(team, taps, gw, rank_ref, bc_ref, dt_ref, *refs):
    got = refs[: team - 1]
    halo_ref, shift_ref, docs_ref, wb_b_ref, wb_c_ref, heads_ref = refs[team - 1 : team + 5]
    s_ref, bt_ref, cm_ref, uv_ref, row_ref, raw_ref, b_ref, sems = refs[team + 5 :]
    rank = rank_ref[0]
    tiles = SPAN // LANES
    own_heads = LANES // team
    half = bc_ref.shape[1] // 2
    b_at = pl.multiple_of(rank * STATE, LANES)
    c_at = pl.multiple_of(half + rank * STATE, LANES)
    own = [(bc_ref.at[:, pl.ds(b_at, STATE)], 0), (bc_ref.at[:, pl.ds(c_at, STATE)], STATE), (dt_ref, 2 * STATE)]
    others = [[(ref.at[:, 0 : 2 * STATE + LANES], 0)] for ref in got]
    gather_rows(rank, [own] + others, raw_ref, halo_ref[:, gw : gw + 2 * STATE], sems)

    lane = iota((LANES, LANES), 1)
    part = lane // own_heads

    def mine(value):
        near = part[: value.shape[0]]
        moved = pltpu.roll(value, (LANES - rank * own_heads) % LANES, 1)
        kept = jnp.where(near == 0, moved, 0.0)
        total = kept
        for step in range(1, team):
            total = total + pltpu.roll(kept, step * own_heads, 1)
        return total

    heads = mine(heads_ref[...])
    bias_row, skip_row = heads[0:1], heads[2:3]
    decay_row = -jnp.exp(heads[1:2])
    ones = jnp.where(iota((LANES, LANES), 0) >= lane, 1.0, 0.0)

    last_doc = docs_ref[0:1, LANES + SPAN - 1 : LANES + SPAN]
    prev_doc = docs_ref[0:1, LANES - 1 : LANES]
    start = jnp.zeros((1, LANES), F32)
    rows_g, rows_e = [], []
    for a in range(tiles):
        here = slice(a * LANES, (a + 1) * LANES)
        raw = raw_ref[a * LANES : (a + 2) * LANES, :]
        shift = shift_ref[a]
        b_tile = conv_tile(raw[:, 0:STATE], shift, [wb_b_ref[i : i + 1, :] for i in range(taps)], wb_b_ref[taps : taps + 1, :])
        c_tile = conv_tile(raw[:, STATE : 2 * STATE], shift, [wb_c_ref[i : i + 1, :] for i in range(taps)], wb_c_ref[taps : taps + 1, :])
        b_ref[here, :] = b_tile
        own = column_of(docs_ref[0:1, (a + 1) * LANES : (a + 2) * LANES])
        own_two = jnp.concatenate([own, own], axis=1)
        cm_ref[here, :] = jnp.where(own_two == prev_doc, c_tile.astype(F32), 0.0).astype(BF16)
        masked = jnp.where(own_two == last_doc, b_tile.astype(F32), 0.0)
        bt_ref[:, here] = jnp.transpose(masked).astype(BF16)
        for b in range(a + 1):
            there = slice(b * LANES, (b + 1) * LANES)
            scores = lax.dot_general(
                c_tile, b_ref[there, :], (((1,), (1,)), ((), ())), preferred_element_type=F32
            )
            keep = own == docs_ref[0:1, (b + 1) * LANES : (b + 2) * LANES]
            if a == b:
                keep = keep & (iota((LANES, LANES), 0) >= lane)
            s_ref[here, there] = jnp.where(keep, scores, 0.0).astype(BF16)
        raised = mine(raw[LANES:, 2 * STATE : 2 * STATE + LANES].astype(F32)) + bias_row
        step = jnp.maximum(raised, 0.0) + jnp.log1p(jnp.exp(-jnp.abs(raised)))
        cum = jnp.dot(ones, decay_row * step, precision=lax.Precision.HIGHEST, preferred_element_type=F32)
        u_hi, u_lo = split_hi(jnp.exp(cum))
        v_hi, v_lo = split_hi(jnp.exp(-cum) * step)
        packed = jnp.where(part == 0, v_hi, jnp.where(part == 1, v_lo, jnp.where(part == 2, u_hi, u_lo)))
        uv_ref[here, :] = packed.astype(BF16)
        tile_total = cum[LANES - 1 : LANES]
        rows_g.append(jnp.exp(tile_total))
        rows_e.append(jnp.exp(start))
        start = start + tile_total
    passes = jnp.exp(start) * jnp.where(last_doc == prev_doc, 1.0, 0.0)
    every = rows_g + rows_e + [skip_row, passes] + [jnp.zeros((1, LANES), F32)] * 6
    hi, lo = split_hi(jnp.concatenate(every, axis=0))
    near = part[: 16]
    row_ref[...] = jnp.where(near == 0, hi, jnp.where(near == 1, lo, 0.0)).astype(BF16)


def spreader(first, width, hdim, own_heads, upper):
    row, col = iota((LANES, width), 0), iota((LANES, width), 1)
    hit = (row % own_heads) == (first + col // hdim)
    half = (row >= 2 * own_heads) if upper else (row < 2 * own_heads)
    return jnp.where(hit & half, 1.0, 0.0).astype(BF16)


def mix_kernel(team, taps, hdim, gw, start, places, rank_ref, *refs):
    x_ref = refs[0]
    got = refs[1:team]
    halo_ref, shift_ref, wb_ref, s_ref, bt_ref, uv_ref, row_ref = refs[team : team + 7]
    xc_ref, yl_ref, st_ref, raw_ref, xf_ref, xb_ref, sems = refs[-7:]
    rank = rank_ref[0]
    tiles = SPAN // LANES
    width = xc_ref.shape[1]
    own_heads = LANES // team
    first = start // hdim
    cols = slice(start, start + width)
    at = pl.multiple_of(rank * gw + start, LANES)
    sources = [[(x_ref.at[:, pl.ds(at, width)], 0)]]
    for ref, place in zip(got, places):
        sources.append([(ref.at[:, place : place + width], 0)])
    gather_rows(rank, sources, raw_ref, halo_ref[:, cols], sems)
    spread_v = spreader(first, width, hdim, own_heads, False)
    spread_u = spreader(first, width, hdim, own_heads, True)
    rows = jnp.dot(row_ref[...], spread_v, preferred_element_type=F32)
    skip = rows[2 * tiles : 2 * tiles + 1]
    weights = [wb_ref[i : i + 1, cols] for i in range(taps)]
    bias = wb_ref[taps : taps + 1, cols]
    for a in range(tiles):
        here = slice(a * LANES, (a + 1) * LANES)
        xc = conv_tile(raw_ref[a * LANES : (a + 2) * LANES, :], shift_ref[a], weights, bias)
        xc_ref[here, :] = xc
        xf = xc.astype(F32)
        uv = uv_ref[here, :]
        scaled = jnp.dot(uv, spread_v, preferred_element_type=F32) * xf
        xf_ref[here, :] = scaled
        xb_ref[here, :] = scaled.astype(BF16)
        total = jnp.dot(
            s_ref[here, 0 : (a + 1) * LANES], xb_ref[0 : (a + 1) * LANES, :], preferred_element_type=F32
        )
        yl_ref[here, :] = jnp.dot(uv, spread_u, preferred_element_type=F32) * total + skip * xf
        for b in range(a + 1):
            there = slice(b * LANES, (b + 1) * LANES)
            later = xf_ref[there, :] * rows[a : a + 1]
            if a < tiles - 1:
                xf_ref[there, :] = later
            xb_ref[there, :] = later.astype(BF16)
    st_ref[...] = jnp.dot(bt_ref[...], xb_ref[...], preferred_element_type=F32).astype(BF16)


def carry_kernel(team, start, hdim, rank_ref, st_ref, yl_ref, xc_ref, cm_ref, uv_ref, row_ref, docs_ref, *refs):
    own_ref, near_ref, far_ref, across_ref, stat_ref, rows_ref, held_ref, sem = refs[-8:]
    first = start // hdim
    rank = rank_ref[0]
    tiles = SPAN // LANES
    width = xc_ref.shape[1]
    own_heads = LANES // team
    spread_v = spreader(first, width, hdim, own_heads, False)
    spread_u = spreader(first, width, hdim, own_heads, True)
    rows_ref[...] = jnp.dot(row_ref[...], spread_v, preferred_element_type=F32)
    stat_refs = refs[1:2] if start else []
    sums = jnp.zeros((DOCS, 3 * LANES), F32)
    for k in (1, 2, 3, 0):
        tile = rank ^ k
        here = pl.ds(pl.multiple_of(tile * LANES, LANES), LANES)
        came = jnp.dot(cm_ref[here, :], st_ref[...], preferred_element_type=F32)
        decay = jnp.dot(uv_ref[here, :], spread_u, preferred_element_type=F32)
        y = yl_ref[here, :] + decay * (came * rows_ref[pl.ds(tiles + tile, 1), :])
        y = y.astype(BF16)
        if k == 1:
            held_ref[...] = y
            near = pltpu.make_async_copy(held_ref, near_ref.at[:, start : start + width], sem)
            near.start()
        else:
            (own_ref, None, far_ref, across_ref)[k][...] = y
        y = y.astype(F32)
        x = xc_ref[here, :].astype(F32)
        parts = []
        for product in (y * x, y * y, x * x):
            part = product[:, 0:LANES]
            for c in range(1, width // LANES):
                part = part + product[:, c * LANES : (c + 1) * LANES]
            parts.append(part)
        docs = docs_ref[0:1, pl.ds(pl.multiple_of((tile + 1) * LANES, LANES), LANES)]
        table = jnp.where(iota((DOCS, LANES), 0).astype(F32) == docs, 1.0, 0.0)
        sums = sums + jnp.dot(
            table, jnp.concatenate(parts, axis=1), precision=lax.Precision.HIGHEST, preferred_element_type=F32
        )
    lane = iota((DOCS, LANES), 1)
    out = jnp.zeros((DOCS, LANES), F32)
    for i in range(3):
        out = jnp.where(lane == i, jnp.sum(sums[:, i * LANES : (i + 1) * LANES], axis=1, keepdims=True), out)
    for ref in stat_refs:
        out = out + ref[...]
    stat_ref[...] = out
    near.wait()


def add_kernel(rank_ref, one_ref, other_ref, *refs):
    refs[-1][...] = one_ref[...] + other_ref[...]


def norm_kernel(blocks, rank_ref, *refs):
    y_count = sum(len(block) for block in blocks)
    z_ref, gain_ref = refs[y_count : y_count + 2]
    out_ref, done_ref, gated_ref = refs[-3:]
    width = z_ref.shape[1]
    done_ref[...] = jnp.zeros_like(done_ref)
    for step, block in enumerate(blocks):

        @pl.when(pl.program_id(0) == step)
        def _():
            part = jnp.zeros((LANES, LANES), F32)
            done = 0
            for at in block:
                y_ref = refs[at]
                size = y_ref.shape[1]
                cols = slice(done, done + size)
                gated = y_ref[...].astype(F32) * silu(z_ref[:, cols].astype(F32))
                gated_ref[:, cols] = gated
                square = gated * gated
                for c in range(size // LANES):
                    part = part + square[:, c * LANES : (c + 1) * LANES]
                done += size
            scale = lax.rsqrt(jnp.sum(part, axis=1, keepdims=True) * (1.0 / width) + 1e-05)
            for c in range(width // (4 * LANES)):
                cols = slice(c * 4 * LANES, (c + 1) * 4 * LANES)
                out_ref[:, cols] = (gated_ref[:, cols] * scale * gain_ref[0:1, cols]).astype(BF16)


def on_device(
    x_stream,
    bc_stream,
    z_stream,
    dt_raw,
    doc_ids,
    conv_weight,
    conv_bias,
    dt_bias,
    a_log,
    skip_d,
    norm_gain,
):
    rows, inner = x_stream.shape
    heads = dt_raw.shape[1]
    hdim = inner // heads
    taps = conv_weight.shape[0]
    members = lax.axis_size("seq")
    team = SPAN // rows
    tiles = SPAN // LANES
    gw = inner // team
    chunks = [gw // 8 * part for part in PARTS]
    me = lax.axis_index("seq")
    rank = jnp.reshape(me % team, (1,)).astype(jnp.int32)
    doc_most = rows * members // 4
    hops = (doc_most - 2) // SPAN + 1

    def swap(array, k):
        return lax.ppermute(array, "seq", [(i, i ^ k) for i in range(members)])

    def onward(array):
        return lax.ppermute(array, "seq", [(i, (i + team) % members) for i in range(members)])

    shape = jax.ShapeDtypeStruct
    bcd_w = 2 * STATE + LANES
    lead_w = bcd_w + gw * HALO // rows
    widths = [bcd_w] * 2 + [lead_w + gw]
    halo_shape = (HALO, gw + 2 * STATE)
    packed = call(
        functools.partial(pack_kernel, team, gw),
        rank,
        (x_stream, bc_stream, dt_raw),
        [ANY] * 3,
        [shape((rows, width), BF16) for width in widths] + [shape(halo_shape, BF16)] * 3,
        [ANY] * (len(widths) + 3),
        [
            pltpu.VMEM((rows, gw), BF16),
            pltpu.VMEM((HALO, inner), BF16),
            pltpu.VMEM(bc_stream.shape, BF16),
            pltpu.VMEM(dt_raw.shape, BF16),
            pltpu.SemaphoreType.DMA((4,)),
            pltpu.SemaphoreType.DMA((9 + rows // HALO + 1 + 9,)),
        ],
        "pack",
        cost=cost(2),
        limit=VMEM_MOST,
    )
    near = swap(packed[2], 1)
    lead = [near, swap(packed[0], 2), swap(packed[1], 3)]
    x_parts = call(
        functools.partial(chunk_kernel, chunks, gw),
        rank,
        (x_stream, near),
        [ANY] * 2,
        [shape((rows, size), BF16) for size in chunks for _ in range(2)],
        [ANY] * (2 * len(chunks)),
        [
            pltpu.VMEM((2, rows, gw), BF16),
            pltpu.SemaphoreType.DMA((2,)),
            pltpu.SemaphoreType.DMA((2 * len(chunks),)),
        ],
        "chunks",
        cost=cost(2),
    )
    got = [[near, swap(x_parts[2 * q], 2), swap(x_parts[2 * q + 1], 3)] for q in range(len(chunks))]

    ext_docs = jnp.concatenate([jnp.full((LANES,), -1, jnp.int32), doc_ids])
    docs = lax.dynamic_slice_in_dim(ext_docs, (me // team) * SPAN, SPAN + LANES).astype(F32)[None]
    wb = jnp.concatenate([conv_weight, conv_bias[None]], axis=0)
    head_rows = jnp.concatenate(
        [dt_bias[None], a_log[None], skip_d[None], jnp.zeros((5, heads), F32)], axis=0
    )
    shift_shape = (tiles, (taps - 1) * LANES, 2 * LANES)
    shift = call(
        functools.partial(shift_kernel, taps),
        rank,
        (docs,),
        [whole(docs.shape)],
        shape(shift_shape, BF16),
        whole(shift_shape),
        [],
        "shift",
        cost=cost(1.5),
    )
    halo = onward(
        call(
            functools.partial(relay_kernel, team, gw),
            rank,
            (packed[5], near, swap(packed[3], 2), swap(packed[4], 3)),
            [ANY] * 4,
            shape(halo_shape, BF16),
            whole(halo_shape),
            [pltpu.SemaphoreType.DMA((1 + rows // HALO,))],
            "relay",
            cost=cost(1),
        )
    )

    b_block, c_block = inner // STATE, inner // STATE + team
    scores, b_turned, c_masked, uv, row_pack = call(
        functools.partial(bc_kernel, team, taps, gw),
        rank,
        (bc_stream, dt_raw, *lead, halo, shift, docs, wb, wb, head_rows),
        [ANY] * 2
        + [ANY] * (team - 1)
        + [
            whole(halo_shape),
            whole(shift_shape),
            whole(docs.shape),
            pl.BlockSpec((taps + 1, STATE), lambda i, pref: (0, b_block + pref[0])),
            pl.BlockSpec((taps + 1, STATE), lambda i, pref: (0, c_block + pref[0])),
            whole(head_rows.shape),
        ],
        [
            shape((SPAN, SPAN), BF16),
            shape((STATE, SPAN), BF16),
            shape((SPAN, STATE), BF16),
            shape((SPAN, LANES), BF16),
            shape((16, LANES), BF16),
        ],
        [
            whole((SPAN, SPAN)),
            whole((STATE, SPAN)),
            whole((SPAN, STATE)),
            whole((SPAN, LANES)),
            whole((16, LANES)),
        ],
        [
            pltpu.VMEM((LANES + SPAN, bcd_w), BF16),
            pltpu.VMEM((SPAN, STATE), BF16),
            pltpu.SemaphoreType.DMA((team + 2,)),
        ],
        "bc",
        cost=cost(4),
    )

    def mix(q, after):
        start, size = sum(chunks[:q]), chunks[q]
        xc, y_local, fresh = call(
            functools.partial(mix_kernel, team, taps, hdim, gw, start, (lead_w + start, 0, 0)),
            rank,
            (x_stream, *got[q], halo, shift, wb, scores, b_turned, uv, row_pack, *after),
            [ANY]
            + [ANY] * (team - 1)
            + [
                whole(halo_shape),
                whole(shift_shape),
                pl.BlockSpec((taps + 1, gw), lambda i, pref: (0, pref[0])),
                whole((SPAN, SPAN)),
                whole((STATE, SPAN)),
                whole((SPAN, LANES)),
                whole((16, LANES)),
            ]
            + [ANY] * len(after),
            [shape((SPAN, size), BF16), shape((SPAN, size), F32), shape((STATE, size), BF16)],
            [whole((SPAN, size)), whole((SPAN, size)), whole((STATE, size))],
            [
                pltpu.VMEM((LANES + SPAN, size), BF16),
                pltpu.VMEM((SPAN, size), F32),
                pltpu.VMEM((SPAN, size), BF16),
                pltpu.SemaphoreType.DMA((team,)),
            ],
            "mix",
            cost=cost(4),
        )
        state = onward(fresh)
        if hops > 1:
            first, count, own_heads = start // hdim, size // hdim, heads // team
            part = row_pack[2 * tiles + 1].astype(F32)
            kept = part[first : first + count] + part[own_heads + first : own_heads + first + count]
            kept = jnp.repeat(kept, hdim)[None]
            for _ in range(hops - 1):
                state = onward((fresh.astype(F32) + kept * state.astype(F32)).astype(BF16))
        return state, y_local, xc

    def carry(q, mixed, y_near, stats, after):
        start, size = sum(chunks[:q]), chunks[q]
        before = [y_near, stats] if q else []
        return call(
            functools.partial(carry_kernel, team, start, hdim),
            rank,
            (*mixed, c_masked, uv, row_pack, docs, *before, *after),
            [
                whole((STATE, size)),
                whole((SPAN, size)),
                whole((SPAN, size)),
                whole((SPAN, STATE)),
                whole((SPAN, LANES)),
                whole((16, LANES)),
                whole(docs.shape),
            ]
            + ([ANY, whole((DOCS, LANES))] if q else [])
            + [ANY] * len(after),
            [shape((rows, size), BF16), shape((rows, gw), BF16)]
            + [shape((rows, size), BF16)] * 2
            + [shape((DOCS, LANES), F32)],
            [whole((rows, size)), ANY, whole((rows, size)), whole((rows, size)), whole((DOCS, LANES))],
            [pltpu.VMEM((16, size), F32), pltpu.VMEM((rows, size), BF16), pltpu.SemaphoreType.DMA],
            "carry",
            cost=cost(3),
            aliases={8: 1} if q else {},
        )

    y_own, y_far, y_across, stats, y_near = [], [], [], None, None
    ready = [mix(0, []), mix(1, [])]
    for q in range(len(chunks)):
        after = [y_far[q - 1], y_across[q - 1]] if q else []
        own, y_near, far, across, stats = carry(q, ready[q], y_near, stats, after)
        y_own.append(own)
        y_far.append(swap(far, 2))
        y_across.append(swap(across, 3))
        if q + 2 < len(chunks):
            ready.append(mix(q + 2, [stats]))
    y_near = swap(y_near, 1)

    gain = norm_gain[None]

    def norm(blocks, first, before):
        parts = [array for block in blocks for array in block]
        places, done = [], 0
        for block in blocks:
            places.append(list(range(done, done + len(block))))
            done += len(block)
        place = pl.BlockSpec((rows, gw), lambda i, pref: (0, pref[0] ^ (first + i)))
        return call(
            functools.partial(norm_kernel, places),
            rank,
            (*parts, z_stream, gain, *before),
            [whole(array.shape) for array in parts]
            + [place, pl.BlockSpec((1, gw), lambda i, pref: (0, pref[0] ^ (first + i)))]
            + [ANY] * len(before),
            [shape((rows, inner), BF16), shape((8, LANES), F32)],
            [place, whole((8, LANES))],
            [pltpu.VMEM((rows, gw), F32)],
            "norm",
            grid=(len(blocks),),
            cost=cost(2),
            aliases={len(parts) + 3: 0} if before else {},
        )

    mixed, near_done = norm([y_own, [y_near]], 0, [])
    mixed, far_done = norm([y_far, y_across], 2, [mixed])

    steps = [1 << place for place in range((members - 1).bit_length())]
    within = (team - 1).bit_length()
    flips = steps[within:] + steps[:within]
    for i, flip in enumerate(flips):
        came = swap(stats, flip)
        after = {len(flips) - 3: [near_done], len(flips) - 2: [far_done]}.get(i, [])
        if after:
            stats = call(
                add_kernel,
                rank,
                (stats, came, *after),
                [whole((DOCS, LANES))] * 2 + [ANY] * len(after),
                shape((DOCS, LANES), F32),
                whole((DOCS, LANES)),
                [],
                "add",
                cost=cost(0.1),
            )
        else:
            stats = stats + came
    doc_cosine = stats[:, 0] / jnp.sqrt(stats[:, 1] * stats[:, 2] + 1e-06)
    return (mixed, doc_cosine)


def solution(mesh):
    return jax.shard_map(
        on_device,
        mesh=mesh,
        in_specs=(
            P(("groups", "seq"), None),
            P(("groups", "seq"), None),
            P(("groups", "seq"), None),
            P(("groups", "seq"), None),
            P("groups"),
            P(),
            P(),
            P(),
            P(),
            P(),
            P(),
        ),
        out_specs=(P(("groups", "seq"), None), P("groups")),
        check_vma=False,
    )
```

```python
import functools

import jax
import jax.numpy as jnp
from jax import lax
from jax.experimental import pallas as pl
from jax.experimental.pallas import tpu as pltpu
from jax.sharding import PartitionSpec as P

STATE = 256
SPAN = 512
DOCS = 16
HALO = 16
PARTS = (2, 3, 3)
LANES = 128
VMEM_LIMIT = 20 * 1024 * 1024
VMEM_MOST = 60 * 1024 * 1024

F32 = jnp.float32
BF16 = jnp.bfloat16
ANY = pl.BlockSpec(memory_space=pl.ANY)


def iota(shape, dim):
    return lax.broadcasted_iota(jnp.int32, shape, dim)


def whole(shape):
    return pl.BlockSpec(shape, lambda i, pref: (0,) * len(shape))


def call(kernel, rank, inputs, in_specs, out_shapes, out_specs, scratch, name, grid=(1,), cost=None, aliases={}, limit=VMEM_LIMIT):
    return pl.pallas_call(
        kernel,
        grid_spec=pltpu.PrefetchScalarGridSpec(
            num_scalar_prefetch=1,
            grid=grid,
            in_specs=in_specs,
            out_specs=out_specs,
            scratch_shapes=scratch,
        ),
        out_shape=out_shapes,
        compiler_params=pltpu.CompilerParams(vmem_limit_bytes=limit),
        cost_estimate=cost,
        input_output_aliases=aliases,
        name=name,
    )(rank, *inputs)


def cost(us):
    return pl.CostEstimate(flops=int(us * 1e9), bytes_accessed=int(us * 3e6), transcendentals=0)


def halve(x, b, c):
    full = jnp.concatenate([part.astype(F32)[HALO // 2 :] for part in (x, b, c)], axis=1)
    width = full.shape[1] // 2
    return jnp.concatenate([full[:, :width], full[:, width:]], axis=0).astype(BF16)


def whole_halo(halo):
    half = HALO // 2
    full = jnp.concatenate([halo.astype(F32)[:half], halo.astype(F32)[half:]], axis=1)
    return jnp.concatenate([jnp.zeros_like(full), full], axis=0).astype(BF16)


def pack_kernel(team, gw, rank_ref, x_ref, bc_ref, dt_ref, *refs):
    xv_ref, tail_ref, bcv_ref, dtv_ref, held_ref, in_sems, out_sems = refs[-7:]
    outs = list(refs[:-7])
    rank = rank_ref[0]
    rows = x_ref.shape[0]
    half = bc_ref.shape[1] // 2
    last = pl.ds(rows - HALO, HALO)

    def fetch(src, dst, sem):
        made = pltpu.make_async_copy(src, dst, in_sems.at[sem])
        made.start()
        return made

    fetches = [
        fetch(bc_ref, bcv_ref, 0),
        fetch(dt_ref, dtv_ref, 1),
        fetch(x_ref.at[last], tail_ref, 2),
        fetch(x_ref.at[:, pl.ds(pl.multiple_of((rank ^ 1) * gw, LANES), gw)], xv_ref, 3),
    ]
    copies = []

    def copy(src, dst):
        made = pltpu.make_async_copy(src, dst, out_sems.at[len(copies)])
        made.start()
        copies.append(made)

    for made in fetches[:3]:
        made.wait()
    for k in (2, 3, 1):
        out = outs.pop(0)
        at = pl.multiple_of((rank ^ k) * STATE, STATE)
        copy(bcv_ref.at[:, pl.ds(at, STATE)], out.at[:, 0:STATE])
        at = pl.multiple_of(half + (rank ^ k) * STATE, STATE)
        copy(bcv_ref.at[:, pl.ds(at, STATE)], out.at[:, STATE : 2 * STATE])
        copy(dtv_ref, out.at[:, 2 * STATE : 2 * STATE + LANES])
    first = 2 * STATE + LANES
    for i, k in enumerate((2, 3, 0)):
        at = pl.multiple_of((rank ^ k) * gw, LANES)
        b_at = pl.multiple_of((rank ^ k) * STATE, LANES)
        c_at = pl.multiple_of(half + (rank ^ k) * STATE, LANES)
        held_ref[i] = halve(
            tail_ref[:, pl.ds(at, gw)], bcv_ref[last, pl.ds(b_at, STATE)], bcv_ref[last, pl.ds(c_at, STATE)]
        )
        copy(held_ref.at[i], outs.pop(0))
    fetches[3].wait()
    copy(xv_ref, out.at[:, first : first + gw])
    for made in copies:
        made.wait()


def chunk_kernel(chunks, start, gw, rank_ref, x_ref, after_ref, *refs):
    xv_ref, in_sems, out_sems = refs[-3:]
    outs = list(refs[:-3])
    rank = rank_ref[0]
    fetches, copies = [], []
    for i, k in enumerate((2, 3)):
        at = pl.multiple_of((rank ^ k) * gw + start, LANES)
        made = pltpu.make_async_copy(x_ref.at[:, pl.ds(at, sum(chunks))], xv_ref.at[i], in_sems.at[i])
        made.start()
        fetches.append(made)
    for made in fetches:
        made.wait()
    done = 0
    for size in chunks:
        for i in range(2):
            src = xv_ref.at[i, :, pl.ds(done, size)]
            made = pltpu.make_async_copy(src, outs.pop(0), out_sems.at[len(copies)])
            made.start()
            copies.append(made)
        done += size
    for made in copies:
        made.wait()


def relay_kernel(team, gw, rank_ref, tail_ref, near_ref, *refs):
    others = {0: tail_ref, 2: refs[0], 3: refs[1]}
    out_ref, near_tail_ref, sem = refs[-3:]
    rank = rank_ref[0]
    rows = near_ref.shape[0]

    def copy(src, dst):
        made = pltpu.make_async_copy(src, dst, sem)
        made.start()
        made.wait()

    for k, ref in others.items():

        @pl.when(rank ^ k == team - 1)
        def _():
            copy(ref, out_ref)

    @pl.when(rank ^ 1 == team - 1)
    def _():
        copy(near_ref.at[pl.ds(rows - HALO, HALO)], near_tail_ref)
        first = 2 * STATE + LANES
        out_ref[...] = halve(
            near_tail_ref[:, first : first + gw],
            near_tail_ref[:, 0:STATE],
            near_tail_ref[:, STATE : 2 * STATE],
        )


def column_of(row):
    return jnp.transpose(jnp.broadcast_to(row, (LANES, row.shape[1])))


def shift_kernel(taps, rank_ref, docs_ref, shift_ref):
    tiles = shift_ref.shape[0]
    for a in range(tiles):
        near = docs_ref[0:1, a * LANES : (a + 2) * LANES]
        own = column_of(docs_ref[0:1, (a + 1) * LANES : (a + 2) * LANES])
        same = jnp.concatenate([own, own], axis=1) == near
        row, col = iota((LANES, 2 * LANES), 0), iota((LANES, 2 * LANES), 1)
        for back in range(1, taps):
            hit = same & (col == row + (LANES - back))
            shift_ref[a, (back - 1) * LANES : back * LANES, :] = jnp.where(hit, 1.0, 0.0).astype(BF16)


def gather_rows(rank, sources, raw_ref, halo, sems):
    copies = []
    for k, parts in enumerate(sources):
        at = pl.multiple_of(LANES + (rank ^ k) * LANES, LANES)
        for source, first in parts:
            dst = raw_ref.at[pl.ds(at, LANES), first : first + source.shape[1]]
            made = pltpu.make_async_copy(source, dst, sems.at[len(copies)])
            made.start()
            copies.append(made)
    width = halo.shape[1]
    raw_ref[0 : LANES - HALO, 0:width] = jnp.zeros((LANES - HALO, width), BF16)
    raw_ref[LANES - HALO : LANES, 0:width] = halo
    for made in copies:
        made.wait()


def silu(value):
    half = 0.5 * value
    return half + half * jnp.tanh(half)


def conv_tile(raw, shift, taps, bias):
    count = len(taps)
    moved = jnp.dot(shift, raw, preferred_element_type=F32)
    total = raw[LANES:].astype(F32) * taps[count - 1] + bias
    for back in range(1, count):
        total = total + moved[(back - 1) * LANES : back * LANES] * taps[count - 1 - back]
    return silu(total).astype(BF16)


def split_hi(value):
    hi = value.astype(BF16).astype(F32)
    return hi, value - hi


def bc_kernel(team, taps, gw, rank_ref, bc_ref, dt_ref, *refs):
    got = refs[: team - 1]
    halo_ref, shift_ref, docs_ref, wb_b_ref, wb_c_ref, heads_ref = refs[team - 1 : team + 5]
    s_ref, bt_ref, cm_ref, uv_ref, row_ref, raw_ref, b_ref, sems = refs[team + 5 :]
    rank = rank_ref[0]
    tiles = SPAN // LANES
    own_heads = LANES // team
    half = bc_ref.shape[1] // 2
    b_at = pl.multiple_of(rank * STATE, LANES)
    c_at = pl.multiple_of(half + rank * STATE, LANES)
    own = [(bc_ref.at[:, pl.ds(b_at, STATE)], 0), (bc_ref.at[:, pl.ds(c_at, STATE)], STATE), (dt_ref, 2 * STATE)]
    others = [[(ref.at[:, 0 : 2 * STATE + LANES], 0)] for ref in got]
    gather_rows(rank, [own] + others, raw_ref, whole_halo(halo_ref[...])[:, gw : gw + 2 * STATE], sems)

    lane = iota((LANES, LANES), 1)
    part = lane // own_heads

    def mine(value):
        near = part[: value.shape[0]]
        moved = pltpu.roll(value, (LANES - rank * own_heads) % LANES, 1)
        kept = jnp.where(near == 0, moved, 0.0)
        total = kept
        for step in range(1, team):
            total = total + pltpu.roll(kept, step * own_heads, 1)
        return total

    heads = mine(heads_ref[...])
    bias_row, skip_row = heads[0:1], heads[2:3]
    decay_row = -jnp.exp(heads[1:2])
    ones = jnp.where(iota((LANES, LANES), 0) >= lane, 1.0, 0.0)

    last_doc = docs_ref[0:1, LANES + SPAN - 1 : LANES + SPAN]
    prev_doc = docs_ref[0:1, LANES - 1 : LANES]
    start = jnp.zeros((1, LANES), F32)
    rows_g, rows_e = [], []
    for a in range(tiles):
        here = slice(a * LANES, (a + 1) * LANES)
        raw = raw_ref[a * LANES : (a + 2) * LANES, :]
        shift = shift_ref[a]
        b_tile = conv_tile(raw[:, 0:STATE], shift, [wb_b_ref[i : i + 1, :] for i in range(taps)], wb_b_ref[taps : taps + 1, :])
        c_tile = conv_tile(raw[:, STATE : 2 * STATE], shift, [wb_c_ref[i : i + 1, :] for i in range(taps)], wb_c_ref[taps : taps + 1, :])
        b_ref[here, :] = b_tile
        own = column_of(docs_ref[0:1, (a + 1) * LANES : (a + 2) * LANES])
        own_two = jnp.concatenate([own, own], axis=1)
        cm_ref[here, :] = jnp.where(own_two == prev_doc, c_tile.astype(F32), 0.0).astype(BF16)
        masked = jnp.where(own_two == last_doc, b_tile.astype(F32), 0.0)
        bt_ref[:, here] = jnp.transpose(masked).astype(BF16)
        for b in range(a + 1):
            there = slice(b * LANES, (b + 1) * LANES)
            scores = lax.dot_general(
                c_tile, b_ref[there, :], (((1,), (1,)), ((), ())), preferred_element_type=F32
            )
            keep = own == docs_ref[0:1, (b + 1) * LANES : (b + 2) * LANES]
            if a == b:
                keep = keep & (iota((LANES, LANES), 0) >= lane)
            s_ref[here, there] = jnp.where(keep, scores, 0.0).astype(BF16)
        raised = mine(raw[LANES:, 2 * STATE : 2 * STATE + LANES].astype(F32)) + bias_row
        step = jnp.maximum(raised, 0.0) + jnp.log1p(jnp.exp(-jnp.abs(raised)))
        cum = jnp.dot(ones, decay_row * step, precision=lax.Precision.HIGHEST, preferred_element_type=F32)
        u_hi, u_lo = split_hi(jnp.exp(cum))
        v_hi, v_lo = split_hi(jnp.exp(-cum) * step)
        packed = jnp.where(part == 0, v_hi, jnp.where(part == 1, v_lo, jnp.where(part == 2, u_hi, u_lo)))
        uv_ref[here, :] = packed.astype(BF16)
        tile_total = cum[LANES - 1 : LANES]
        rows_g.append(jnp.exp(tile_total))
        rows_e.append(jnp.exp(start))
        start = start + tile_total
    passes = jnp.exp(start) * jnp.where(last_doc == prev_doc, 1.0, 0.0)
    every = rows_g + rows_e + [skip_row, passes] + [jnp.zeros((1, LANES), F32)] * 6
    hi, lo = split_hi(jnp.concatenate(every, axis=0))
    near = part[: 16]
    row_ref[...] = jnp.where(near == 0, hi, jnp.where(near == 1, lo, 0.0)).astype(BF16)


def spreader(first, width, hdim, own_heads, upper):
    row, col = iota((LANES, width), 0), iota((LANES, width), 1)
    hit = (row % own_heads) == (first + col // hdim)
    half = (row >= 2 * own_heads) if upper else (row < 2 * own_heads)
    return jnp.where(hit & half, 1.0, 0.0).astype(BF16)


def mix_kernel(team, taps, hdim, gw, start, places, rank_ref, *refs):
    x_ref = refs[0]
    got = refs[1:team]
    halo_ref, shift_ref, wb_ref, s_ref, bt_ref, uv_ref, row_ref = refs[team : team + 7]
    xc_ref, yl_ref, st_ref, raw_ref, xf_ref, xb_ref, sems = refs[-7:]
    rank = rank_ref[0]
    tiles = SPAN // LANES
    width = xc_ref.shape[1]
    own_heads = LANES // team
    first = start // hdim
    cols = slice(start, start + width)
    at = pl.multiple_of(rank * gw + start, LANES)
    sources = [[(x_ref.at[:, pl.ds(at, width)], 0)]]
    for ref, place in zip(got, places):
        sources.append([(ref.at[:, place : place + width], 0)])
    gather_rows(rank, sources, raw_ref, whole_halo(halo_ref[...])[:, cols], sems)
    spread_v = spreader(first, width, hdim, own_heads, False)
    spread_u = spreader(first, width, hdim, own_heads, True)
    rows = jnp.dot(row_ref[...], spread_v, preferred_element_type=F32)
    skip = rows[2 * tiles : 2 * tiles + 1]
    weights = [wb_ref[i : i + 1, cols] for i in range(taps)]
    bias = wb_ref[taps : taps + 1, cols]
    for a in range(tiles):
        here = slice(a * LANES, (a + 1) * LANES)
        xc = conv_tile(raw_ref[a * LANES : (a + 2) * LANES, :], shift_ref[a], weights, bias)
        xc_ref[here, :] = xc
        xf = xc.astype(F32)
        uv = uv_ref[here, :]
        scaled = jnp.dot(uv, spread_v, preferred_element_type=F32) * xf
        xf_ref[here, :] = scaled
        xb_ref[here, :] = scaled.astype(BF16)
        total = jnp.dot(
            s_ref[here, 0 : (a + 1) * LANES], xb_ref[0 : (a + 1) * LANES, :], preferred_element_type=F32
        )
        yl_ref[here, :] = jnp.dot(uv, spread_u, preferred_element_type=F32) * total + skip * xf
        for b in range(a + 1):
            there = slice(b * LANES, (b + 1) * LANES)
            later = xf_ref[there, :] * rows[a : a + 1]
            if a < tiles - 1:
                xf_ref[there, :] = later
            xb_ref[there, :] = later.astype(BF16)
    st_ref[...] = jnp.dot(bt_ref[...], xb_ref[...], preferred_element_type=F32).astype(BF16)


def carry_kernel(team, start, hdim, rank_ref, st_ref, yl_ref, xc_ref, cm_ref, uv_ref, row_ref, docs_ref, *refs):
    own_ref, near_ref, far_ref, across_ref, stat_ref, rows_ref, held_ref, sem = refs[-8:]
    first = start // hdim
    rank = rank_ref[0]
    tiles = SPAN // LANES
    width = xc_ref.shape[1]
    own_heads = LANES // team
    spread_v = spreader(first, width, hdim, own_heads, False)
    spread_u = spreader(first, width, hdim, own_heads, True)
    rows_ref[...] = jnp.dot(row_ref[...], spread_v, preferred_element_type=F32)
    stat_refs = refs[1:2] if start else []
    sums = jnp.zeros((DOCS, 3 * LANES), F32)
    for k in (1, 2, 3, 0):
        tile = rank ^ k
        here = pl.ds(pl.multiple_of(tile * LANES, LANES), LANES)
        came = jnp.dot(cm_ref[here, :], st_ref[...], preferred_element_type=F32)
        decay = jnp.dot(uv_ref[here, :], spread_u, preferred_element_type=F32)
        y = yl_ref[here, :] + decay * (came * rows_ref[pl.ds(tiles + tile, 1), :])
        y = y.astype(BF16)
        if k == 1:
            held_ref[...] = y
            near = pltpu.make_async_copy(held_ref, near_ref.at[:, start : start + width], sem)
            near.start()
        else:
            (own_ref, None, far_ref, across_ref)[k][...] = y
        y = y.astype(F32)
        x = xc_ref[here, :].astype(F32)
        parts = []
        for product in (y * x, y * y, x * x):
            part = product[:, 0:LANES]
            for c in range(1, width // LANES):
                part = part + product[:, c * LANES : (c + 1) * LANES]
            parts.append(part)
        docs = docs_ref[0:1, pl.ds(pl.multiple_of((tile + 1) * LANES, LANES), LANES)]
        table = jnp.where(iota((DOCS, LANES), 0).astype(F32) == docs, 1.0, 0.0)
        sums = sums + jnp.dot(
            table, jnp.concatenate(parts, axis=1), precision=lax.Precision.HIGHEST, preferred_element_type=F32
        )
    lane = iota((DOCS, LANES), 1)
    out = jnp.zeros((DOCS, LANES), F32)
    for i in range(3):
        out = jnp.where(lane == i, jnp.sum(sums[:, i * LANES : (i + 1) * LANES], axis=1, keepdims=True), out)
    for ref in stat_refs:
        out = out + ref[...]
    stat_ref[...] = out
    near.wait()


def add_kernel(rank_ref, one_ref, other_ref, after_ref, out_ref):
    out_ref[...] = one_ref[...] + other_ref[...]


def norm_kernel(blocks, rank_ref, *refs):
    y_count = sum(len(block) for block in blocks)
    z_ref, gain_ref = refs[y_count : y_count + 2]
    out_ref, done_ref, gated_ref = refs[-3:]
    width = z_ref.shape[1]
    done_ref[...] = jnp.zeros_like(done_ref)
    for step, block in enumerate(blocks):

        @pl.when(pl.program_id(0) == step)
        def _():
            part = jnp.zeros((LANES, LANES), F32)
            done = 0
            for at in block:
                y_ref = refs[at]
                size = y_ref.shape[1]
                cols = slice(done, done + size)
                gated = y_ref[...].astype(F32) * silu(z_ref[:, cols].astype(F32))
                gated_ref[:, cols] = gated
                square = gated * gated
                for c in range(size // LANES):
                    part = part + square[:, c * LANES : (c + 1) * LANES]
                done += size
            scale = lax.rsqrt(jnp.sum(part, axis=1, keepdims=True) * (1.0 / width) + 1e-05)
            for c in range(width // (4 * LANES)):
                cols = slice(c * 4 * LANES, (c + 1) * 4 * LANES)
                out_ref[:, cols] = (gated_ref[:, cols] * scale * gain_ref[0:1, cols]).astype(BF16)


def on_device(
    x_stream,
    bc_stream,
    z_stream,
    dt_raw,
    doc_ids,
    conv_weight,
    conv_bias,
    dt_bias,
    a_log,
    skip_d,
    norm_gain,
):
    rows, inner = x_stream.shape
    heads = dt_raw.shape[1]
    hdim = inner // heads
    taps = conv_weight.shape[0]
    members = lax.axis_size("seq")
    team = SPAN // rows
    tiles = SPAN // LANES
    gw = inner // team
    chunks = [gw // 8 * part for part in PARTS]
    me = lax.axis_index("seq")
    rank = jnp.reshape(me % team, (1,)).astype(jnp.int32)
    doc_most = rows * members // 4
    hops = (doc_most - 2) // SPAN + 1

    def swap(array, k):
        return lax.ppermute(array, "seq", [(i, i ^ k) for i in range(members)])

    def onward(array):
        return lax.ppermute(array, "seq", [(i, (i + team) % members) for i in range(members)])

    shape = jax.ShapeDtypeStruct
    bcd_w = 2 * STATE + LANES
    widths = [bcd_w] * 2 + [bcd_w + gw]
    halo_shape = (HALO, gw // 2 + STATE)
    packed = call(
        functools.partial(pack_kernel, team, gw),
        rank,
        (x_stream, bc_stream, dt_raw),
        [ANY] * 3,
        [shape((rows, width), BF16) for width in widths] + [shape(halo_shape, BF16)] * 3,
        [ANY] * (len(widths) + 3),
        [
            pltpu.VMEM((rows, gw), BF16),
            pltpu.VMEM((HALO, inner), BF16),
            pltpu.VMEM(bc_stream.shape, BF16),
            pltpu.VMEM(dt_raw.shape, BF16),
            pltpu.VMEM((3, *halo_shape), BF16),
            pltpu.SemaphoreType.DMA((4,)),
            pltpu.SemaphoreType.DMA((13,)),
        ],
        "pack",
        cost=cost(2),
        limit=VMEM_MOST,
    )
    near = swap(packed[2], 1)
    lead = [near, swap(packed[0], 2), swap(packed[1], 3)]
    def send_chunks(first, count, after):
        sizes = chunks[first : first + count]
        parts = call(
            functools.partial(chunk_kernel, sizes, sum(chunks[:first]), gw),
            rank,
            (x_stream, after),
            [ANY] * 2,
            [shape((rows, size), BF16) for size in sizes for _ in range(2)],
            [ANY] * (2 * count),
            [
                pltpu.VMEM((2, rows, sum(sizes)), BF16),
                pltpu.SemaphoreType.DMA((2,)),
                pltpu.SemaphoreType.DMA((2 * count,)),
            ],
            "chunks",
            cost=cost(1),
        )
        return [[near, swap(parts[2 * q], 2), swap(parts[2 * q + 1], 3)] for q in range(count)]

    got = send_chunks(0, len(chunks) - 1, near)

    ext_docs = jnp.concatenate([jnp.full((LANES,), -1, jnp.int32), doc_ids])
    docs = lax.dynamic_slice_in_dim(ext_docs, (me // team) * SPAN, SPAN + LANES).astype(F32)[None]
    wb = jnp.concatenate([conv_weight, conv_bias[None]], axis=0)
    head_rows = jnp.concatenate(
        [dt_bias[None], a_log[None], skip_d[None], jnp.zeros((5, heads), F32)], axis=0
    )
    shift_shape = (tiles, (taps - 1) * LANES, 2 * LANES)
    shift = call(
        functools.partial(shift_kernel, taps),
        rank,
        (docs,),
        [whole(docs.shape)],
        shape(shift_shape, BF16),
        whole(shift_shape),
        [],
        "shift",
        cost=cost(1.5),
    )
    halo = onward(
        call(
            functools.partial(relay_kernel, team, gw),
            rank,
            (packed[5], near, swap(packed[3], 2), swap(packed[4], 3)),
            [ANY] * 4,
            shape(halo_shape, BF16),
            whole(halo_shape),
            [pltpu.VMEM((HALO, bcd_w + gw), BF16), pltpu.SemaphoreType.DMA],
            "relay",
            cost=cost(1),
        )
    )

    b_block, c_block = inner // STATE, inner // STATE + team
    scores, b_turned, c_masked, uv, row_pack = call(
        functools.partial(bc_kernel, team, taps, gw),
        rank,
        (bc_stream, dt_raw, *lead, halo, shift, docs, wb, wb, head_rows),
        [ANY] * 2
        + [ANY] * (team - 1)
        + [
            whole(halo_shape),
            whole(shift_shape),
            whole(docs.shape),
            pl.BlockSpec((taps + 1, STATE), lambda i, pref: (0, b_block + pref[0])),
            pl.BlockSpec((taps + 1, STATE), lambda i, pref: (0, c_block + pref[0])),
            whole(head_rows.shape),
        ],
        [
            shape((SPAN, SPAN), BF16),
            shape((STATE, SPAN), BF16),
            shape((SPAN, STATE), BF16),
            shape((SPAN, LANES), BF16),
            shape((16, LANES), BF16),
        ],
        [
            whole((SPAN, SPAN)),
            whole((STATE, SPAN)),
            whole((SPAN, STATE)),
            whole((SPAN, LANES)),
            whole((16, LANES)),
        ],
        [
            pltpu.VMEM((LANES + SPAN, bcd_w), BF16),
            pltpu.VMEM((SPAN, STATE), BF16),
            pltpu.SemaphoreType.DMA((team + 2,)),
        ],
        "bc",
        cost=cost(4),
    )

    def mix(q, after):
        start, size = sum(chunks[:q]), chunks[q]
        xc, y_local, fresh = call(
            functools.partial(mix_kernel, team, taps, hdim, gw, start, (bcd_w + start, 0, 0)),
            rank,
            (x_stream, *got[q], halo, shift, wb, scores, b_turned, uv, row_pack, *after),
            [ANY]
            + [ANY] * (team - 1)
            + [
                whole(halo_shape),
                whole(shift_shape),
                pl.BlockSpec((taps + 1, gw), lambda i, pref: (0, pref[0])),
                whole((SPAN, SPAN)),
                whole((STATE, SPAN)),
                whole((SPAN, LANES)),
                whole((16, LANES)),
            ]
            + [ANY] * len(after),
            [shape((SPAN, size), BF16), shape((SPAN, size), F32), shape((STATE, size), BF16)],
            [whole((SPAN, size)), whole((SPAN, size)), whole((STATE, size))],
            [
                pltpu.VMEM((LANES + SPAN, size), BF16),
                pltpu.VMEM((SPAN, size), F32),
                pltpu.VMEM((SPAN, size), BF16),
                pltpu.SemaphoreType.DMA((team,)),
            ],
            "mix",
            cost=cost(4),
        )
        if q == 0:
            got.extend(send_chunks(len(chunks) - 1, 1, fresh))
        state = onward(fresh)
        if hops > 1:
            first, count, own_heads = start // hdim, size // hdim, heads // team
            part = row_pack[2 * tiles + 1].astype(F32)
            kept = part[first : first + count] + part[own_heads + first : own_heads + first + count]
            kept = jnp.repeat(kept, hdim)[None]
            for _ in range(hops - 1):
                state = onward((fresh.astype(F32) + kept * state.astype(F32)).astype(BF16))
        return state, y_local, xc

    def carry(q, mixed, y_near, stats, after):
        start, size = sum(chunks[:q]), chunks[q]
        before = [y_near, stats] if q else []
        return call(
            functools.partial(carry_kernel, team, start, hdim),
            rank,
            (*mixed, c_masked, uv, row_pack, docs, *before, *after),
            [
                whole((STATE, size)),
                whole((SPAN, size)),
                whole((SPAN, size)),
                whole((SPAN, STATE)),
                whole((SPAN, LANES)),
                whole((16, LANES)),
                whole(docs.shape),
            ]
            + ([ANY, whole((DOCS, LANES))] if q else [])
            + [ANY] * len(after),
            [shape((rows, size), BF16), shape((rows, gw), BF16)]
            + [shape((rows, size), BF16)] * 2
            + [shape((DOCS, LANES), F32)],
            [whole((rows, size)), ANY, whole((rows, size)), whole((rows, size)), whole((DOCS, LANES))],
            [pltpu.VMEM((16, size), F32), pltpu.VMEM((rows, size), BF16), pltpu.SemaphoreType.DMA],
            "carry",
            cost=cost(3),
            aliases={8: 1} if q else {},
        )

    y_own, y_far, y_across, stats, y_near = [], [], [], None, None
    ready = [mix(0, []), mix(1, [])]
    for q in range(len(chunks)):
        after = [y_far[q - 1], y_across[q - 1]] if q else []
        own, y_near, far, across, stats = carry(q, ready[q], y_near, stats, after)
        y_own.append(own)
        y_far.append(swap(far, 2))
        y_across.append(swap(across, 3))
        if q + 2 < len(chunks):
            ready.append(mix(q + 2, [stats]))
    y_near = swap(y_near, 1)

    gain = norm_gain[None]

    def norm(blocks, first, before):
        parts = [array for block in blocks for array in block]
        places, done = [], 0
        for block in blocks:
            places.append(list(range(done, done + len(block))))
            done += len(block)
        place = pl.BlockSpec((rows, gw), lambda i, pref: (0, pref[0] ^ (first + i)))
        return call(
            functools.partial(norm_kernel, places),
            rank,
            (*parts, z_stream, gain, *before),
            [whole(array.shape) for array in parts]
            + [place, pl.BlockSpec((1, gw), lambda i, pref: (0, pref[0] ^ (first + i)))]
            + [ANY] * len(before),
            [shape((rows, inner), BF16), shape((8, LANES), F32)],
            [place, whole((8, LANES))],
            [pltpu.VMEM((rows, gw), F32)],
            "norm",
            grid=(len(blocks),),
            cost=cost(2),
            aliases={len(parts) + 3: 0} if before else {},
        )

    mixed, near_done = norm([y_own, [y_near]], 0, [])
    mixed, _ = norm([y_far, y_across], 2, [mixed])

    steps = [1 << place for place in range((members - 1).bit_length())]
    within = (team - 1).bit_length()
    for i, flip in enumerate(steps[within:] + steps[:within]):
        came = swap(stats, flip)
        if i == 1:
            stats = call(
                add_kernel,
                rank,
                (stats, came, near_done),
                [whole((DOCS, LANES))] * 2 + [ANY],
                shape((DOCS, LANES), F32),
                whole((DOCS, LANES)),
                [],
                "add",
                cost=cost(0.1),
            )
        else:
            stats = stats + came
    doc_cosine = stats[:, 0] / jnp.sqrt(stats[:, 1] * stats[:, 2] + 1e-06)
    return (mixed, doc_cosine)


def solution(mesh):
    return jax.shard_map(
        on_device,
        mesh=mesh,
        in_specs=(
            P(("groups", "seq"), None),
            P(("groups", "seq"), None),
            P(("groups", "seq"), None),
            P(("groups", "seq"), None),
            P("groups"),
            P(),
            P(),
            P(),
            P(),
            P(),
            P(),
        ),
        out_specs=(P(("groups", "seq"), None), P("groups")),
        check_vma=False,
    )
```

```python
import functools

import jax
import jax.numpy as jnp
from jax import lax
from jax.experimental import pallas as pl
from jax.experimental.pallas import tpu as pltpu
from jax.sharding import PartitionSpec as P

STATE = 256
SPAN = 512
DOCS = 16
HALO = 16
PARTS = (4, 5, 7)
LANES = 128
VMEM_LIMIT = 20 * 1024 * 1024
VMEM_MOST = 60 * 1024 * 1024

F32 = jnp.float32
BF16 = jnp.bfloat16
ANY = pl.BlockSpec(memory_space=pl.ANY)


def iota(shape, dim):
    return lax.broadcasted_iota(jnp.int32, shape, dim)


def whole(shape):
    return pl.BlockSpec(shape, lambda i, pref: (0,) * len(shape))


def call(kernel, rank, inputs, in_specs, out_shapes, out_specs, scratch, name, grid=(1,), cost=None, aliases={}, limit=VMEM_LIMIT):
    return pl.pallas_call(
        kernel,
        grid_spec=pltpu.PrefetchScalarGridSpec(
            num_scalar_prefetch=1,
            grid=grid,
            in_specs=in_specs,
            out_specs=out_specs,
            scratch_shapes=scratch,
        ),
        out_shape=out_shapes,
        compiler_params=pltpu.CompilerParams(vmem_limit_bytes=limit),
        cost_estimate=cost,
        input_output_aliases=aliases,
        name=name,
    )(rank, *inputs)


def cost(us):
    return pl.CostEstimate(flops=int(us * 1e9), bytes_accessed=int(us * 3e6), transcendentals=0)


def halve(x, b, c):
    full = jnp.concatenate([part.astype(F32)[HALO // 2 :] for part in (x, b, c)], axis=1)
    width = full.shape[1] // 2
    return jnp.concatenate([full[:, :width], full[:, width:]], axis=0).astype(BF16)


def whole_halo(halo):
    half = HALO // 2
    full = jnp.concatenate([halo.astype(F32)[:half], halo.astype(F32)[half:]], axis=1)
    return jnp.concatenate([jnp.zeros_like(full), full], axis=0).astype(BF16)


def pack_kernel(team, gw, rank_ref, x_ref, bc_ref, dt_ref, *refs):
    xv_ref, tail_ref, bcv_ref, dtv_ref, held_ref, in_sems, out_sems = refs[-7:]
    outs = list(refs[:-7])
    rank = rank_ref[0]
    rows = x_ref.shape[0]
    half = bc_ref.shape[1] // 2
    last = pl.ds(rows - HALO, HALO)

    def fetch(src, dst, sem):
        made = pltpu.make_async_copy(src, dst, in_sems.at[sem])
        made.start()
        return made

    fetches = [
        fetch(bc_ref, bcv_ref, 0),
        fetch(dt_ref, dtv_ref, 1),
        fetch(x_ref.at[last], tail_ref, 2),
        fetch(x_ref.at[:, pl.ds(pl.multiple_of((rank ^ 1) * gw, LANES), gw)], xv_ref, 3),
    ]
    copies = []

    def copy(src, dst):
        made = pltpu.make_async_copy(src, dst, out_sems.at[len(copies)])
        made.start()
        copies.append(made)

    for made in fetches[:3]:
        made.wait()
    for k in (2, 3, 1):
        out = outs.pop(0)
        at = pl.multiple_of((rank ^ k) * STATE, STATE)
        copy(bcv_ref.at[:, pl.ds(at, STATE)], out.at[:, 0:STATE])
        at = pl.multiple_of(half + (rank ^ k) * STATE, STATE)
        copy(bcv_ref.at[:, pl.ds(at, STATE)], out.at[:, STATE : 2 * STATE])
        copy(dtv_ref, out.at[:, 2 * STATE : 2 * STATE + LANES])
    first = 2 * STATE + LANES
    for i, k in enumerate((2, 3, 0)):
        at = pl.multiple_of((rank ^ k) * gw, LANES)
        b_at = pl.multiple_of((rank ^ k) * STATE, LANES)
        c_at = pl.multiple_of(half + (rank ^ k) * STATE, LANES)
        held_ref[i] = halve(
            tail_ref[:, pl.ds(at, gw)], bcv_ref[last, pl.ds(b_at, STATE)], bcv_ref[last, pl.ds(c_at, STATE)]
        )
        copy(held_ref.at[i], outs.pop(0))
    fetches[3].wait()
    copy(xv_ref, out.at[:, first : first + gw])
    for made in copies:
        made.wait()


def chunk_kernel(chunks, start, gw, rank_ref, x_ref, after_ref, *refs):
    xv_ref, in_sems, out_sems = refs[-3:]
    outs = list(refs[:-3])
    rank = rank_ref[0]
    fetches, copies = [], []
    for i, k in enumerate((2, 3)):
        at = pl.multiple_of((rank ^ k) * gw + start, LANES)
        made = pltpu.make_async_copy(x_ref.at[:, pl.ds(at, sum(chunks))], xv_ref.at[i], in_sems.at[i])
        made.start()
        fetches.append(made)
    for made in fetches:
        made.wait()
    done = 0
    for size in chunks:
        for i in range(2):
            src = xv_ref.at[i, :, pl.ds(done, size)]
            made = pltpu.make_async_copy(src, outs.pop(0), out_sems.at[len(copies)])
            made.start()
            copies.append(made)
        done += size
    for made in copies:
        made.wait()


def relay_kernel(team, gw, rank_ref, tail_ref, near_ref, *refs):
    others = {0: tail_ref, 2: refs[0], 3: refs[1]}
    out_ref, near_tail_ref, sem = refs[-3:]
    rank = rank_ref[0]
    rows = near_ref.shape[0]

    def copy(src, dst):
        made = pltpu.make_async_copy(src, dst, sem)
        made.start()
        made.wait()

    for k, ref in others.items():

        @pl.when(rank ^ k == team - 1)
        def _():
            copy(ref, out_ref)

    @pl.when(rank ^ 1 == team - 1)
    def _():
        copy(near_ref.at[pl.ds(rows - HALO, HALO)], near_tail_ref)
        first = 2 * STATE + LANES
        out_ref[...] = halve(
            near_tail_ref[:, first : first + gw],
            near_tail_ref[:, 0:STATE],
            near_tail_ref[:, STATE : 2 * STATE],
        )


def column_of(row):
    return jnp.transpose(jnp.broadcast_to(row, (LANES, row.shape[1])))


def shift_kernel(taps, rank_ref, docs_ref, shift_ref):
    tiles = shift_ref.shape[0]
    for a in range(tiles):
        near = docs_ref[0:1, a * LANES : (a + 2) * LANES]
        own = column_of(docs_ref[0:1, (a + 1) * LANES : (a + 2) * LANES])
        same = jnp.concatenate([own, own], axis=1) == near
        row, col = iota((LANES, 2 * LANES), 0), iota((LANES, 2 * LANES), 1)
        for back in range(1, taps):
            hit = same & (col == row + (LANES - back))
            shift_ref[a, (back - 1) * LANES : back * LANES, :] = jnp.where(hit, 1.0, 0.0).astype(BF16)


def gather_rows(rank, sources, raw_ref, halo, sems):
    copies = []
    for k, parts in enumerate(sources):
        at = pl.multiple_of(LANES + (rank ^ k) * LANES, LANES)
        for source, first in parts:
            dst = raw_ref.at[pl.ds(at, LANES), first : first + source.shape[1]]
            made = pltpu.make_async_copy(source, dst, sems.at[len(copies)])
            made.start()
            copies.append(made)
    width = halo.shape[1]
    raw_ref[0 : LANES - HALO, 0:width] = jnp.zeros((LANES - HALO, width), BF16)
    raw_ref[LANES - HALO : LANES, 0:width] = halo
    for made in copies:
        made.wait()


def silu(value):
    half = 0.5 * value
    return half + half * jnp.tanh(half)


def conv_tile(raw, shift, taps, bias):
    count = len(taps)
    moved = jnp.dot(shift, raw, preferred_element_type=F32)
    total = raw[LANES:].astype(F32) * taps[count - 1] + bias
    for back in range(1, count):
        total = total + moved[(back - 1) * LANES : back * LANES] * taps[count - 1 - back]
    return silu(total).astype(BF16)


def split_hi(value):
    hi = value.astype(BF16).astype(F32)
    return hi, value - hi


def bc_kernel(team, taps, gw, rank_ref, bc_ref, dt_ref, *refs):
    got = refs[: team - 1]
    halo_ref, shift_ref, docs_ref, wb_b_ref, wb_c_ref, heads_ref = refs[team - 1 : team + 5]
    s_ref, bt_ref, cm_ref, uv_ref, row_ref, raw_ref, b_ref, sems = refs[team + 5 :]
    rank = rank_ref[0]
    tiles = SPAN // LANES
    own_heads = LANES // team
    half = bc_ref.shape[1] // 2
    b_at = pl.multiple_of(rank * STATE, LANES)
    c_at = pl.multiple_of(half + rank * STATE, LANES)
    own = [(bc_ref.at[:, pl.ds(b_at, STATE)], 0), (bc_ref.at[:, pl.ds(c_at, STATE)], STATE), (dt_ref, 2 * STATE)]
    others = [[(ref.at[:, 0 : 2 * STATE + LANES], 0)] for ref in got]
    gather_rows(rank, [own] + others, raw_ref, whole_halo(halo_ref[...])[:, gw : gw + 2 * STATE], sems)

    lane = iota((LANES, LANES), 1)
    part = lane // own_heads

    def mine(value):
        near = part[: value.shape[0]]
        moved = pltpu.roll(value, (LANES - rank * own_heads) % LANES, 1)
        kept = jnp.where(near == 0, moved, 0.0)
        total = kept
        for step in range(1, team):
            total = total + pltpu.roll(kept, step * own_heads, 1)
        return total

    heads = mine(heads_ref[...])
    bias_row, skip_row = heads[0:1], heads[2:3]
    decay_row = -jnp.exp(heads[1:2])
    ones = jnp.where(iota((LANES, LANES), 0) >= lane, 1.0, 0.0)

    last_doc = docs_ref[0:1, LANES + SPAN - 1 : LANES + SPAN]
    prev_doc = docs_ref[0:1, LANES - 1 : LANES]
    start = jnp.zeros((1, LANES), F32)
    rows_g, rows_e = [], []
    for a in range(tiles):
        here = slice(a * LANES, (a + 1) * LANES)
        raw = raw_ref[a * LANES : (a + 2) * LANES, :]
        shift = shift_ref[a]
        b_tile = conv_tile(raw[:, 0:STATE], shift, [wb_b_ref[i : i + 1, :] for i in range(taps)], wb_b_ref[taps : taps + 1, :])
        c_tile = conv_tile(raw[:, STATE : 2 * STATE], shift, [wb_c_ref[i : i + 1, :] for i in range(taps)], wb_c_ref[taps : taps + 1, :])
        b_ref[here, :] = b_tile
        own = column_of(docs_ref[0:1, (a + 1) * LANES : (a + 2) * LANES])
        own_two = jnp.concatenate([own, own], axis=1)
        cm_ref[here, :] = jnp.where(own_two == prev_doc, c_tile.astype(F32), 0.0).astype(BF16)
        masked = jnp.where(own_two == last_doc, b_tile.astype(F32), 0.0)
        bt_ref[:, here] = jnp.transpose(masked).astype(BF16)
        for b in range(a + 1):
            there = slice(b * LANES, (b + 1) * LANES)
            scores = lax.dot_general(
                c_tile, b_ref[there, :], (((1,), (1,)), ((), ())), preferred_element_type=F32
            )
            keep = own == docs_ref[0:1, (b + 1) * LANES : (b + 2) * LANES]
            if a == b:
                keep = keep & (iota((LANES, LANES), 0) >= lane)
            s_ref[here, there] = jnp.where(keep, scores, 0.0).astype(BF16)
        raised = mine(raw[LANES:, 2 * STATE : 2 * STATE + LANES].astype(F32)) + bias_row
        step = jnp.maximum(raised, 0.0) + jnp.log1p(jnp.exp(-jnp.abs(raised)))
        cum = jnp.dot(ones, decay_row * step, precision=lax.Precision.HIGHEST, preferred_element_type=F32)
        u_hi, u_lo = split_hi(jnp.exp(cum))
        v_hi, v_lo = split_hi(jnp.exp(-cum) * step)
        packed = jnp.where(part == 0, v_hi, jnp.where(part == 1, v_lo, jnp.where(part == 2, u_hi, u_lo)))
        uv_ref[here, :] = packed.astype(BF16)
        tile_total = cum[LANES - 1 : LANES]
        rows_g.append(jnp.exp(tile_total))
        rows_e.append(jnp.exp(start))
        start = start + tile_total
    passes = jnp.exp(start) * jnp.where(last_doc == prev_doc, 1.0, 0.0)
    every = rows_g + rows_e + [skip_row, passes] + [jnp.zeros((1, LANES), F32)] * 6
    hi, lo = split_hi(jnp.concatenate(every, axis=0))
    near = part[: 16]
    row_ref[...] = jnp.where(near == 0, hi, jnp.where(near == 1, lo, 0.0)).astype(BF16)


def spreader(first, width, hdim, own_heads, upper):
    row, col = iota((LANES, width), 0), iota((LANES, width), 1)
    place = 2 * own_heads if upper else 0
    start = (row - place) * hdim
    start = jnp.where(row >= place + own_heads, start - own_heads * hdim, start) - first * hdim
    inside = (row >= place) & (row < place + 2 * own_heads)
    start = jnp.where(inside, start, 2 * own_heads * hdim)
    return jnp.where((col >= start) & (col < start + hdim), 1.0, 0.0).astype(BF16)


def mix_kernel(team, taps, hdim, gw, start, places, rank_ref, *refs):
    x_ref = refs[0]
    got = refs[1:team]
    halo_ref, shift_ref, wb_ref, s_ref, bt_ref, uv_ref, row_ref = refs[team : team + 7]
    xc_ref, yl_ref, st_ref, raw_ref, xf_ref, xb_ref, sems = refs[-7:]
    rank = rank_ref[0]
    tiles = SPAN // LANES
    width = xc_ref.shape[1]
    own_heads = LANES // team
    first = start // hdim
    cols = slice(start, start + width)
    at = pl.multiple_of(rank * gw + start, LANES)
    sources = [[(x_ref.at[:, pl.ds(at, width)], 0)]]
    for ref, place in zip(got, places):
        sources.append([(ref.at[:, place : place + width], 0)])
    gather_rows(rank, sources, raw_ref, whole_halo(halo_ref[...])[:, cols], sems)
    spread_v = spreader(first, width, hdim, own_heads, False)
    spread_u = spreader(first, width, hdim, own_heads, True)
    rows = jnp.dot(row_ref[...], spread_v, preferred_element_type=F32)
    skip = rows[2 * tiles : 2 * tiles + 1]
    weights = [wb_ref[i : i + 1, cols] for i in range(taps)]
    bias = wb_ref[taps : taps + 1, cols]
    for a in range(tiles):
        here = slice(a * LANES, (a + 1) * LANES)
        xc = conv_tile(raw_ref[a * LANES : (a + 2) * LANES, :], shift_ref[a], weights, bias)
        xc_ref[here, :] = xc
        xf = xc.astype(F32)
        uv = uv_ref[here, :]
        scaled = jnp.dot(uv, spread_v, preferred_element_type=F32) * xf
        xf_ref[here, :] = scaled
        xb_ref[here, :] = scaled.astype(BF16)
        total = jnp.dot(
            s_ref[here, 0 : (a + 1) * LANES], xb_ref[0 : (a + 1) * LANES, :], preferred_element_type=F32
        )
        yl_ref[here, :] = jnp.dot(uv, spread_u, preferred_element_type=F32) * total + skip * xf
        for b in range(a + 1):
            there = slice(b * LANES, (b + 1) * LANES)
            later = xf_ref[there, :] * rows[a : a + 1]
            if a < tiles - 1:
                xf_ref[there, :] = later
            xb_ref[there, :] = later.astype(BF16)
    st_ref[...] = jnp.dot(bt_ref[...], xb_ref[...], preferred_element_type=F32).astype(BF16)


def carry_kernel(team, start, hdim, rank_ref, st_ref, yl_ref, xc_ref, cm_ref, uv_ref, row_ref, docs_ref, *refs):
    own_ref, near_ref, far_ref, across_ref, stat_ref, rows_ref, held_ref, sem = refs[-8:]
    first = start // hdim
    rank = rank_ref[0]
    tiles = SPAN // LANES
    width = xc_ref.shape[1]
    own_heads = LANES // team
    spread_v = spreader(first, width, hdim, own_heads, False)
    spread_u = spreader(first, width, hdim, own_heads, True)
    rows_ref[...] = jnp.dot(row_ref[...], spread_v, preferred_element_type=F32)
    stat_refs = refs[1:2] if start else []
    sums = jnp.zeros((DOCS, 3 * LANES), F32)
    for k in (1, 2, 3, 0):
        tile = rank ^ k
        here = pl.ds(pl.multiple_of(tile * LANES, LANES), LANES)
        came = jnp.dot(cm_ref[here, :], st_ref[...], preferred_element_type=F32)
        decay = jnp.dot(uv_ref[here, :], spread_u, preferred_element_type=F32)
        y = yl_ref[here, :] + decay * (came * rows_ref[pl.ds(tiles + tile, 1), :])
        y = y.astype(BF16)
        if k == 1:
            held_ref[...] = y
            near = pltpu.make_async_copy(held_ref, near_ref.at[:, start : start + width], sem)
            near.start()
        else:
            (own_ref, None, far_ref, across_ref)[k][...] = y
        y = y.astype(F32)
        x = xc_ref[here, :].astype(F32)
        parts = []
        for product in (y * x, y * y, x * x):
            part = product[:, 0:LANES]
            for c in range(1, width // LANES):
                part = part + product[:, c * LANES : (c + 1) * LANES]
            parts.append(part)
        docs = docs_ref[0:1, pl.ds(pl.multiple_of((tile + 1) * LANES, LANES), LANES)]
        table = jnp.where(iota((DOCS, LANES), 0).astype(F32) == docs, 1.0, 0.0)
        sums = sums + jnp.dot(
            table, jnp.concatenate(parts, axis=1), precision=lax.Precision.HIGHEST, preferred_element_type=F32
        )
    lane = iota((DOCS, LANES), 1)
    out = jnp.zeros((DOCS, LANES), F32)
    for i in range(3):
        out = jnp.where(lane == i, jnp.sum(sums[:, i * LANES : (i + 1) * LANES], axis=1, keepdims=True), out)
    for ref in stat_refs:
        out = out + ref[...]
    stat_ref[...] = out
    near.wait()


def add_kernel(rank_ref, one_ref, other_ref, after_ref, out_ref):
    out_ref[...] = one_ref[...] + other_ref[...]


def norm_kernel(blocks, rank_ref, *refs):
    y_count = sum(len(block) for block in blocks)
    z_ref, gain_ref = refs[y_count : y_count + 2]
    out_ref, done_ref, gated_ref = refs[-3:]
    width = z_ref.shape[1]
    done_ref[...] = jnp.zeros_like(done_ref)
    for step, block in enumerate(blocks):

        @pl.when(pl.program_id(0) == step)
        def _():
            part = jnp.zeros((LANES, LANES), F32)
            done = 0
            for at in block:
                y_ref = refs[at]
                size = y_ref.shape[1]
                cols = slice(done, done + size)
                gated = y_ref[...].astype(F32) * silu(z_ref[:, cols].astype(F32))
                gated_ref[:, cols] = gated
                square = gated * gated
                for c in range(size // LANES):
                    part = part + square[:, c * LANES : (c + 1) * LANES]
                done += size
            scale = lax.rsqrt(jnp.sum(part, axis=1, keepdims=True) * (1.0 / width) + 1e-05)
            for c in range(width // (4 * LANES)):
                cols = slice(c * 4 * LANES, (c + 1) * 4 * LANES)
                out_ref[:, cols] = (gated_ref[:, cols] * scale * gain_ref[0:1, cols]).astype(BF16)


def on_device(
    x_stream,
    bc_stream,
    z_stream,
    dt_raw,
    doc_ids,
    conv_weight,
    conv_bias,
    dt_bias,
    a_log,
    skip_d,
    norm_gain,
):
    rows, inner = x_stream.shape
    heads = dt_raw.shape[1]
    hdim = inner // heads
    taps = conv_weight.shape[0]
    members = lax.axis_size("seq")
    team = SPAN // rows
    tiles = SPAN // LANES
    gw = inner // team
    chunks = [gw // 16 * part for part in PARTS]
    me = lax.axis_index("seq")
    rank = jnp.reshape(me % team, (1,)).astype(jnp.int32)
    doc_most = rows * members // 4
    hops = (doc_most - 2) // SPAN + 1

    def swap(array, k):
        return lax.ppermute(array, "seq", [(i, i ^ k) for i in range(members)])

    def onward(array):
        return lax.ppermute(array, "seq", [(i, (i + team) % members) for i in range(members)])

    shape = jax.ShapeDtypeStruct
    bcd_w = 2 * STATE + LANES
    widths = [bcd_w] * 2 + [bcd_w + gw]
    halo_shape = (HALO, gw // 2 + STATE)
    packed = call(
        functools.partial(pack_kernel, team, gw),
        rank,
        (x_stream, bc_stream, dt_raw),
        [ANY] * 3,
        [shape((rows, width), BF16) for width in widths] + [shape(halo_shape, BF16)] * 3,
        [ANY] * (len(widths) + 3),
        [
            pltpu.VMEM((rows, gw), BF16),
            pltpu.VMEM((HALO, inner), BF16),
            pltpu.VMEM(bc_stream.shape, BF16),
            pltpu.VMEM(dt_raw.shape, BF16),
            pltpu.VMEM((3, *halo_shape), BF16),
            pltpu.SemaphoreType.DMA((4,)),
            pltpu.SemaphoreType.DMA((13,)),
        ],
        "pack",
        cost=cost(2),
        limit=VMEM_MOST,
    )
    near = swap(packed[2], 1)
    lead = [near, swap(packed[0], 2), swap(packed[1], 3)]
    def send_chunks(first, count, after):
        sizes = chunks[first : first + count]
        parts = call(
            functools.partial(chunk_kernel, sizes, sum(chunks[:first]), gw),
            rank,
            (x_stream, after),
            [ANY] * 2,
            [shape((rows, size), BF16) for size in sizes for _ in range(2)],
            [ANY] * (2 * count),
            [
                pltpu.VMEM((2, rows, sum(sizes)), BF16),
                pltpu.SemaphoreType.DMA((2,)),
                pltpu.SemaphoreType.DMA((2 * count,)),
            ],
            "chunks",
            cost=cost(1),
        )
        return [[near, swap(parts[2 * q], 2), swap(parts[2 * q + 1], 3)] for q in range(count)]

    got = send_chunks(0, len(chunks) - 1, near)

    ext_docs = jnp.concatenate([jnp.full((LANES,), -1, jnp.int32), doc_ids])
    docs = lax.dynamic_slice_in_dim(ext_docs, (me // team) * SPAN, SPAN + LANES).astype(F32)[None]
    wb = jnp.concatenate([conv_weight, conv_bias[None]], axis=0)
    head_rows = jnp.concatenate(
        [dt_bias[None], a_log[None], skip_d[None], jnp.zeros((5, heads), F32)], axis=0
    )
    shift_shape = (tiles, (taps - 1) * LANES, 2 * LANES)
    shift = call(
        functools.partial(shift_kernel, taps),
        rank,
        (docs,),
        [whole(docs.shape)],
        shape(shift_shape, BF16),
        whole(shift_shape),
        [],
        "shift",
        cost=cost(1.5),
    )
    halo = onward(
        call(
            functools.partial(relay_kernel, team, gw),
            rank,
            (packed[5], near, swap(packed[3], 2), swap(packed[4], 3)),
            [ANY] * 4,
            shape(halo_shape, BF16),
            whole(halo_shape),
            [pltpu.VMEM((HALO, bcd_w + gw), BF16), pltpu.SemaphoreType.DMA],
            "relay",
            cost=cost(1),
        )
    )

    b_block, c_block = inner // STATE, inner // STATE + team
    scores, b_turned, c_masked, uv, row_pack = call(
        functools.partial(bc_kernel, team, taps, gw),
        rank,
        (bc_stream, dt_raw, *lead, halo, shift, docs, wb, wb, head_rows),
        [ANY] * 2
        + [ANY] * (team - 1)
        + [
            whole(halo_shape),
            whole(shift_shape),
            whole(docs.shape),
            pl.BlockSpec((taps + 1, STATE), lambda i, pref: (0, b_block + pref[0])),
            pl.BlockSpec((taps + 1, STATE), lambda i, pref: (0, c_block + pref[0])),
            whole(head_rows.shape),
        ],
        [
            shape((SPAN, SPAN), BF16),
            shape((STATE, SPAN), BF16),
            shape((SPAN, STATE), BF16),
            shape((SPAN, LANES), BF16),
            shape((16, LANES), BF16),
        ],
        [
            whole((SPAN, SPAN)),
            whole((STATE, SPAN)),
            whole((SPAN, STATE)),
            whole((SPAN, LANES)),
            whole((16, LANES)),
        ],
        [
            pltpu.VMEM((LANES + SPAN, bcd_w), BF16),
            pltpu.VMEM((SPAN, STATE), BF16),
            pltpu.SemaphoreType.DMA((team + 2,)),
        ],
        "bc",
        cost=cost(4),
    )

    def mix(q, after):
        start, size = sum(chunks[:q]), chunks[q]
        xc, y_local, fresh = call(
            functools.partial(mix_kernel, team, taps, hdim, gw, start, (bcd_w + start, 0, 0)),
            rank,
            (x_stream, *got[q], halo, shift, wb, scores, b_turned, uv, row_pack, *after),
            [ANY]
            + [ANY] * (team - 1)
            + [
                whole(halo_shape),
                whole(shift_shape),
                pl.BlockSpec((taps + 1, gw), lambda i, pref: (0, pref[0])),
                whole((SPAN, SPAN)),
                whole((STATE, SPAN)),
                whole((SPAN, LANES)),
                whole((16, LANES)),
            ]
            + [ANY] * len(after),
            [shape((SPAN, size), BF16), shape((SPAN, size), F32), shape((STATE, size), BF16)],
            [whole((SPAN, size)), whole((SPAN, size)), whole((STATE, size))],
            [
                pltpu.VMEM((LANES + SPAN, size), BF16),
                pltpu.VMEM((SPAN, size), F32),
                pltpu.VMEM((SPAN, size), BF16),
                pltpu.SemaphoreType.DMA((team,)),
            ],
            "mix",
            cost=cost(4),
        )
        if q == 0:
            got.extend(send_chunks(len(chunks) - 1, 1, fresh))
        state = onward(fresh)
        if hops > 1:
            first, count, own_heads = start // hdim, size // hdim, heads // team
            part = row_pack[2 * tiles + 1].astype(F32)
            kept = part[first : first + count] + part[own_heads + first : own_heads + first + count]
            kept = jnp.repeat(kept, hdim)[None]
            for _ in range(hops - 1):
                state = onward((fresh.astype(F32) + kept * state.astype(F32)).astype(BF16))
        return state, y_local, xc

    def carry(q, mixed, y_near, stats, after):
        start, size = sum(chunks[:q]), chunks[q]
        before = [y_near, stats] if q else []
        return call(
            functools.partial(carry_kernel, team, start, hdim),
            rank,
            (*mixed, c_masked, uv, row_pack, docs, *before, *after),
            [
                whole((STATE, size)),
                whole((SPAN, size)),
                whole((SPAN, size)),
                whole((SPAN, STATE)),
                whole((SPAN, LANES)),
                whole((16, LANES)),
                whole(docs.shape),
            ]
            + ([ANY, whole((DOCS, LANES))] if q else [])
            + [ANY] * len(after),
            [shape((rows, size), BF16), shape((rows, gw), BF16)]
            + [shape((rows, size), BF16)] * 2
            + [shape((DOCS, LANES), F32)],
            [whole((rows, size)), ANY, whole((rows, size)), whole((rows, size)), whole((DOCS, LANES))],
            [pltpu.VMEM((16, size), F32), pltpu.VMEM((rows, size), BF16), pltpu.SemaphoreType.DMA],
            "carry",
            cost=cost(3),
            aliases={8: 1} if q else {},
        )

    y_own, y_far, y_across, stats, y_near = [], [], [], None, None
    ready = [mix(0, []), mix(1, [])]
    for q in range(len(chunks)):
        after = [y_far[q - 1], y_across[q - 1]] if q else []
        own, y_near, far, across, stats = carry(q, ready[q], y_near, stats, after)
        y_own.append(own)
        y_far.append(swap(far, 2))
        y_across.append(swap(across, 3))
        if q + 2 < len(chunks):
            ready.append(mix(q + 2, [stats]))
    y_near = swap(y_near, 1)

    gain = norm_gain[None]

    def norm(blocks, first, before):
        parts = [array for block in blocks for array in block]
        places, done = [], 0
        for block in blocks:
            places.append(list(range(done, done + len(block))))
            done += len(block)
        place = pl.BlockSpec((rows, gw), lambda i, pref: (0, pref[0] ^ (first + i)))
        return call(
            functools.partial(norm_kernel, places),
            rank,
            (*parts, z_stream, gain, *before),
            [whole(array.shape) for array in parts]
            + [place, pl.BlockSpec((1, gw), lambda i, pref: (0, pref[0] ^ (first + i)))]
            + [ANY] * len(before),
            [shape((rows, inner), BF16), shape((8, LANES), F32)],
            [place, whole((8, LANES))],
            [pltpu.VMEM((rows, gw), F32)],
            "norm",
            grid=(len(blocks),),
            cost=cost(2),
            aliases={len(parts) + 3: 0} if before else {},
        )

    mixed, near_done = norm([y_own, [y_near]], 0, [])
    mixed, _ = norm([y_far, y_across], 2, [mixed])

    steps = [1 << place for place in range((members - 1).bit_length())]
    within = (team - 1).bit_length()
    for i, flip in enumerate(steps[within:] + steps[:within]):
        came = swap(stats, flip)
        if i == 1:
            stats = call(
                add_kernel,
                rank,
                (stats, came, near_done),
                [whole((DOCS, LANES))] * 2 + [ANY],
                shape((DOCS, LANES), F32),
                whole((DOCS, LANES)),
                [],
                "add",
                cost=cost(0.1),
            )
        else:
            stats = stats + came
    doc_cosine = stats[:, 0] / jnp.sqrt(stats[:, 1] * stats[:, 2] + 1e-06)
    return (mixed, doc_cosine)


def solution(mesh):
    return jax.shard_map(
        on_device,
        mesh=mesh,
        in_specs=(
            P(("groups", "seq"), None),
            P(("groups", "seq"), None),
            P(("groups", "seq"), None),
            P(("groups", "seq"), None),
            P("groups"),
            P(),
            P(),
            P(),
            P(),
            P(),
            P(),
        ),
        out_specs=(P(("groups", "seq"), None), P("groups")),
        check_vma=False,
    )
```
